512 devices in a mesh: dp: 64 (over y, z), emb: 8 (over x, core).
Axes of the slice: x: 4, y: 8, z: 8, core: 2. Of those that a mesh axis runs over, the one named last changes fastest.
Arguments:
- actions: bfloat16 [1024, 64, 64], P(('dp', 'emb')), may hold values from -6 to 6
- noise: bfloat16 [1024, 64, 64], P(('dp', 'emb')), may hold values from -6 to 6
- emb_ids: int32 [1024], P(('dp', 'emb')), may hold values from 0 to 23, as said below
- lengths: int32 [1024], P(('dp', 'emb')), may hold values from 16 to 64
- t_index: int32 [1024], P(('dp', 'emb')), may hold values from 0 to 999
- act_dims: int32 [24], replicated, may hold values from 7 to 56
- features: bfloat16 [1024, 8, 5120], P('dp', None, 'emb'), may hold values from -6 to 6
- enc_w: bfloat16 [24, 64, 1536], P('emb'), may hold values from -0.75 to 0.75
- dec_w: bfloat16 [24, 1536, 64], P('emb'), may hold values from -0.15625 to 0.15625
- wq: bfloat16 [1536, 1536], P('dp', 'emb'), may hold values from -0.15625 to 0.15625
- wk: bfloat16 [5120, 1536], P('dp', 'emb'), may hold values from -0.078125 to 0.078125
- wv: bfloat16 [5120, 1536], P('dp', 'emb'), may hold values from -0.078125 to 0.078125
- wo_t: bfloat16 [1536, 1536], P('dp', 'emb'), may hold values from -0.15625 to 0.15625
Outputs:
- d_wq_t: float32 [1536, 1536], P('emb')
- d_wo: float32 [1536, 1536], P('emb')
- loss: float32 [1024], P(('dp', 'emb'))
The draws below stay inside these ranges and needn't reach their ends.
Inputs may be any that keep to these rules, and one draw needn't show every extreme that they name: `emb_ids`: embodiment i belongs to owner i // 3, the index of emb that holds its projectors. Among the 2 spans of one device at most 1 belong to one owner, and in every group of devices along emb some owner gets exactly 1 span from each device of the group.
All inputs are finite; a program needn't handle non-finite values.
Results may differ from the reference program's by a relative error of at most 0.0087.
Values may be sent and summed in bfloat16 or wider, within the bound.
A program may use at most 64 MiB of HBM per device.

```python
import math
import jax
import jax.numpy as jnp
from jax import lax

H = 1536
HEADS = 32
HD = 48
DB = 5120
A = 64
EMB_DEV = 3
STEPS = 64
CTX = 8
CH_DEV = 2
TSTEPS = 1000
EMBODIMENTS = 24
SPANS = 1024
N_EMB = 8


def draw_emb_ids(key, part):
    key = jax.random.fold_in(key, 11)
    key_busy, key_order, key_local = jax.random.split(key, 3)
    owner_count = EMBODIMENTS // EMB_DEV
    groups = SPANS // (CH_DEV * owner_count)
    busy = jax.random.randint(key_busy, (groups, 1, 1), 0, owner_count)
    order_keys = jax.random.split(key_order, groups * owner_count)
    shuffled = jax.vmap(lambda single: jax.random.permutation(single, owner_count - 1) + 1)(order_keys)
    orders = jnp.concatenate([jnp.zeros((groups * owner_count, 1), jnp.int32), shuffled.astype(jnp.int32)], axis=1)
    orders = orders.reshape(groups, owner_count, owner_count)
    position = jnp.arange(CH_DEV) % owner_count
    owners = (busy + orders[:, :, position]) % owner_count
    local = jax.random.randint(key_local, owners.shape, 0, EMB_DEV)
    return (owners * EMB_DEV + local).reshape(SPANS).astype(jnp.int32)


def draw_lengths(key, part):
    key = jax.random.fold_in(key, 12)
    values = jax.random.randint(key, (SPANS,), STEPS // 4, STEPS + 1)
    return values.at[0].set(STEPS).astype(jnp.int32)


def draw_act_dims(key, part):
    key = jax.random.fold_in(key, 13)
    values = jax.random.randint(key, (EMBODIMENTS,), 7, A - 7)
    return values.at[0].set(A - 8).astype(jnp.int32)


def place_ends(values, key, smallest, largest):
    longest = values.shape.index(max(values.shape))
    spots = []
    for shift in (0, 1):
        where = [jax.random.randint(jax.random.fold_in(key, axis), (), 0, length) for axis, length in enumerate(values.shape)]
        where[longest] = (where[longest] + shift) % values.shape[longest]
        spots.append(tuple(where))
    return values.at[spots[0]].set(smallest).at[spots[1]].set(largest)


def shard_levels(rng, shape, cuts, smallest, top_value):
    def one(dim, parts):
        heights = jax.random.uniform(jax.random.fold_in(jax.random.fold_in(rng, 6), dim), (parts,), jnp.float32, smallest / len(cuts), top_value / len(cuts))
        return jnp.repeat(jnp.exp(heights), shape[dim] // parts).reshape((-1,) + (1,) * (len(shape) - dim - 1))

    loudness = one(*cuts[0])
    for cut in cuts[1:]:
        loudness = loudness * one(*cut)
    return loudness


def normal_values(rng, dims, scale, reach, cuts=(), kind=jnp.bfloat16):
    result = scale * jax.random.normal(rng, dims, jnp.float32)
    if cuts:
        result = result * shard_levels(rng, dims, cuts, -0.22, 0.18)
    return jnp.clip(result, -reach, reach).astype(kind)


def setup_inputs(seed: int = 0) -> dict:
    key_of = jax.random.split(jax.random.key(seed), 14)
    return {
        "actions": normal_values(key_of[0], (SPANS, STEPS, A), 1.0, 6.0, ((0, 512),)),
        "noise": normal_values(key_of[1], (SPANS, STEPS, A), 1.0, 6.0, ((0, 512),)),
        "emb_ids": draw_emb_ids(jax.random.fold_in(key_of[13], 71), 0),
        "lengths": draw_lengths(jax.random.fold_in(key_of[13], 71), 0),
        "t_index": place_ends(jax.random.randint(key_of[4], (SPANS,), 0, TSTEPS), jax.random.fold_in(key_of[4], 1), 0, TSTEPS - 1).astype(jnp.int32),
        "act_dims": draw_act_dims(jax.random.fold_in(key_of[13], 71), 0),
        "features": normal_values(key_of[6], (SPANS, CTX, DB), 1.0, 6.0, ((0, 64), (2, 8))),
        "enc_w": normal_values(key_of[7], (EMBODIMENTS, A, H), A ** -0.5, 0.75, ((0, 8),)),
        "dec_w": normal_values(key_of[8], (EMBODIMENTS, H, A), H ** -0.5, 0.15625, ((0, 8),)),
        "wq": normal_values(key_of[9], (H, H), H ** -0.5, 0.15625, ((0, 64), (1, 8))),
        "wk": normal_values(key_of[10], (DB, H), DB ** -0.5, 0.078125, ((0, 64), (1, 8))),
        "wv": normal_values(key_of[11], (DB, H), DB ** -0.5, 0.078125, ((0, 64), (1, 8))),
        "wo_t": normal_values(key_of[12], (H, H), H ** -0.5, 0.15625, ((0, 64), (1, 8))),
    }


def step_embedding(step_values, width):
    half = width // 2
    freq = jnp.exp(-math.log(10000.0) * jnp.arange(half, dtype=jnp.float32) / half)
    angle = step_values.astype(jnp.float32)[:, None] * freq[None, :]
    return jnp.concatenate([jnp.sin(angle), jnp.cos(angle)], axis=1)

def reference(actions, noise, emb_ids, lengths, t_index, act_dims, features, enc_w, dec_w, wq, wk, wv, wo_t):
    group = CH_DEV * N_EMB
    count = SPANS // group
    scale = 1.0 / math.sqrt(HD)

    def one_group(carry, index):
        start = (index * group).astype(jnp.int32)

        def take(array):
            return lax.dynamic_slice_in_dim(array, start, group, 0)
        act_block = take(actions).astype(jnp.float32)
        noise_block = take(noise).astype(jnp.float32)
        ids_block = take(emb_ids)
        length_block = take(lengths)
        level_block = take(t_index)
        fraction = (level_block.astype(jnp.float32) / TSTEPS)[:, None, None]
        noisy = ((1.0 - fraction) * noise_block + fraction * act_block).astype(jnp.bfloat16)
        velocity = act_block - noise_block
        encoded = jnp.einsum('csa,cah->csh', noisy.astype(jnp.float32), enc_w[ids_block].astype(jnp.float32)).astype(jnp.bfloat16)
        hidden = (encoded.astype(jnp.float32) + step_embedding(level_block, H)[:, None, :]).astype(jnp.bfloat16)
        flat_hidden = hidden.reshape(group * STEPS, H)
        queries = jnp.dot(flat_hidden, wq, preferred_element_type=jnp.float32).astype(jnp.bfloat16).reshape(group, STEPS, HEADS, HD)
        feats = take(features).reshape(group * CTX, DB)
        key_heads = jnp.dot(feats, wk, preferred_element_type=jnp.float32).astype(jnp.bfloat16).reshape(group, CTX, HEADS, HD)
        value_heads = jnp.dot(feats, wv, preferred_element_type=jnp.float32).astype(jnp.bfloat16).reshape(group, CTX, HEADS, HD)
        scores = jnp.einsum('gshd,gkhd->ghsk', queries.astype(jnp.float32), key_heads.astype(jnp.float32)) * scale
        raised = jnp.exp(scores)
        probs = raised / lax.optimization_barrier(jnp.sum(raised, axis=-1, keepdims=True))
        attended = jnp.einsum('ghsk,gkhd->gshd', probs.astype(jnp.bfloat16).astype(jnp.float32), value_heads.astype(jnp.float32))
        attended = attended.astype(jnp.bfloat16).reshape(group * STEPS, H)
        mixed = jnp.dot(attended, wo_t.T, preferred_element_type=jnp.float32)
        branch = hidden.astype(jnp.float32) + mixed.reshape(group, STEPS, H)
        dec_block = dec_w[ids_block].astype(jnp.float32)
        predicted = jnp.einsum('csh,cha->csa', branch, dec_block, precision=lax.Precision.HIGHEST)
        dims_block = act_dims[ids_block]
        valid = ((jnp.arange(STEPS)[None, :, None] < length_block[:, None, None]) & (jnp.arange(A)[None, None, :] < dims_block[:, None, None])).astype(jnp.float32)
        error_rows = predicted - velocity
        length_float = length_block.astype(jnp.float32)
        loss_block = lax.optimization_barrier(jnp.sum(valid * error_rows * error_rows, axis=(1, 2))) / length_float
        d_predicted = 2.0 * valid * error_rows / length_float[:, None, None]
        d_branch = jnp.einsum('csa,cha->csh', d_predicted, dec_block, precision=lax.Precision.HIGHEST)
        d_branch = d_branch.astype(jnp.bfloat16).reshape(group * STEPS, H)
        d_out = jnp.dot(attended.T, d_branch, preferred_element_type=jnp.float32)
        d_attended = jnp.dot(d_branch, wo_t, preferred_element_type=jnp.float32).astype(jnp.bfloat16).reshape(group, STEPS, HEADS, HD)
        d_probs = jnp.einsum('gshd,gkhd->ghsk', d_attended.astype(jnp.float32), value_heads.astype(jnp.float32))
        centre = lax.optimization_barrier(jnp.sum(probs * d_probs, axis=-1, keepdims=True))
        d_scores = probs * (d_probs - centre)
        d_queries = (jnp.einsum('ghsk,gkhd->gshd', d_scores, key_heads.astype(jnp.float32)) * scale).astype(jnp.bfloat16)
        d_query_weight = jnp.dot(d_queries.reshape(group * STEPS, H).T, flat_hidden, preferred_element_type=jnp.float32)
        return ((carry[0] + d_query_weight, carry[1] + d_out), loss_block)
    empty = jnp.zeros((H, H), jnp.float32)
    (d_wq_t, d_wo), losses = lax.scan(one_group, (empty, empty), jnp.arange(count, dtype=jnp.int32))
    return (d_wq_t, d_wo, losses.reshape(SPANS))
```

```python
import functools
import math

import jax
import jax.numpy as jnp
from jax import lax
from jax.experimental import pallas as pl
from jax.experimental.pallas import tpu as pltpu
from jax.sharding import PartitionSpec as P

HD = 48
TSTEPS = 1000
H = 1536
HC = 192
STEPS = 64
EMBS = 24
NY = 8
NZ = 8
NX = 4
GROUP = 16
CTX = 8
ROWS = GROUP * STEPS
KA = 64
KB = 48
MESH = pl.DeviceIdType.MESH
BF = jnp.bfloat16
F32 = jnp.float32
NT = (((1,), (1,)), ((), ()))


def mm(a, b):
    return jnp.dot(a, b, preferred_element_type=F32)


def mm_nt(a, b):
    return lax.dot_general(a, b, NT, preferred_element_type=F32)


class Copies:
    def __init__(self, send, recv):
        self.send, self.recv, self.count, self.made = send, recv, 0, []

    def make(self, src, dst, device):
        k = self.count
        self.count += 1
        copy = pltpu.make_async_remote_copy(
            src_ref=src, dst_ref=dst, send_sem=self.send.at[k], recv_sem=self.recv.at[k],
            device_id=device, device_id_type=MESH,
        )
        copy.start()
        self.made.append(copy)
        return copy


N_COPIES = 256


def kernel(
    wa_in, wb_in, f_in, enc_in, dec_in, nz_in, vel_in, meta_in, code_in, ids_in,
    gq_out, go_out, loss_out,
    wa, wb, fg, eg, dg, nzg, cg, ig, ids, kv, qo, wq, wo, kb, vb,
    hid, dbr, prs, att, att_t, dq_t, ps, pr, dp_own, dpg,
    gs, gr, sb, sr, fs, sg, og, send_sems, recv_sems, local_sem,
):
    i = lax.axis_index("dp")
    j = lax.axis_index("emb")
    y, z = i // NZ, i % NZ
    x, c = j // 2, j % 2
    ne = 2 * NX

    barrier = pltpu.get_barrier_semaphore()
    for k in range(1, ne):
        pl.semaphore_signal(barrier, inc=1, device_id=(i, (j + k) % ne), device_id_type=MESH)
    for k in range(1, NY):
        pl.semaphore_signal(barrier, inc=1, device_id=(((y + k) % NY) * NZ + z, j), device_id_type=MESH)
    for k in range(1, NZ):
        pl.semaphore_signal(barrier, inc=1, device_id=(y * NZ + (z + k) % NZ, j), device_id_type=MESH)
    pl.semaphore_wait(barrier, (ne - 1) + (NY - 1) + (NZ - 1))

    cs = Copies(send_sems, recv_sems)
    go = cs.make
    dev_y = lambda t: (t * NZ + z, j)
    dev_z = lambda t: (y * NZ + t, j)
    dev_e = lambda t: (i, t)
    fwd = 1 - 2 * c

    small = []
    for k in range(1, ne):
        peer = dev_e((j + k) % ne)
        small.append(go(nz_in, nzg.at[j], peer))
        small.append(go(code_in, cg.at[j], peer))
        small.append(go(ids_in, ig.at[j], peer))

    def ring(step, me, device, first, block, heavy, light):
        up = device((me + fwd + 8) % 8)
        down = device((me - fwd + 8) % 8)
        out = []
        if step <= heavy:
            b = (me - fwd * (step - 1) + 16) % 8
            for src, dst in zip(first if step == 1 and first else block(b), block(b)):
                out.append(go(src, dst, up))
        if step <= light:
            b = (me + fwd * (step - 1) + 16) % 8
            for src, dst in zip(first if step == 1 and first else block(b), block(b)):
                out.append(go(src, dst, down))
        return out

    def arrive(copies):
        for copy in copies:
            copy.wait_recv()

    a1 = lambda s: ring(s, z, dev_z, [wa_in], lambda b: [wa.at[y, b]], 4, 3)
    b1 = lambda s: ring(s, y, dev_y, [wb_in], lambda b: [wb.at[z, b]], 4, 3)
    a2 = lambda s: ring(s, y, dev_y, None, lambda b: [wa.at[b, pl.ds(0, 4)], wa.at[b, pl.ds(4, 4)]], 4, 3)
    b2 = lambda s: ring(s, z, dev_z, None, lambda b: [wb.at[b, pl.ds(0, 4)], wb.at[b, pl.ds(4, 4)]], 4, 3)

    right, left = (2 * ((x + 1) % NX) + c), (2 * ((x + 3) % NX) + c)
    opposite, sibling = (2 * ((x + 2) % NX) + c), (2 * x + 1 - c)

    def along_x_start(whole_in, half_in, half, whole):
        r0 = go(half_in(0), half(j, 0), dev_e(right))
        l1 = go(half_in(1), half(j, 1), dev_e(left))
        r1 = go(half_in(1), half(j, 1), dev_e(right))
        l0 = go(half_in(0), half(j, 0), dev_e(left))
        s = go(whole_in, whole(j), dev_e(sibling))
        return r0, l1, r1, l0, s

    def along_x_forward(first, half, whole):
        r0, l1, r1, l0, s = first
        r0.wait_recv()
        f0 = go(half(left, 0), half(left, 0), dev_e(right))
        l1.wait_recv()
        f1 = go(half(right, 1), half(right, 1), dev_e(left))
        r1.wait_recv()
        s0 = go(whole(left), whole(left), dev_e(sibling))
        l0.wait_recv()
        s1 = go(whole(right), whole(right), dev_e(sibling))
        return f0, f1, s0, s1, s

    def along_x_last(second, half, whole):
        f0, f1, s0, s1, s = second
        f0.wait_recv()
        f1.wait_recv()
        s2 = go(whole(opposite), whole(opposite), dev_e(sibling))
        return s, s0, s1, s2

    f_half = lambda b, h: fg.at[b, pl.ds(64 * h, 64)]
    f_whole = lambda b: fg.at[b]
    w3 = lambda buf: (
        (lambda b, h: buf.at[pl.ds(3 * b, 3), pl.ds(32 * h, 32)]),
        (lambda b: buf.at[pl.ds(3 * b, 3)]),
    )
    e_half, e_whole = w3(eg)
    d_half, d_whole = w3(dg)

    ra, rb = a1(1), b1(1)
    fx = along_x_start(f_in, lambda h: f_in.at[pl.ds(64 * h, 64)], f_half, f_whole)
    ex = along_x_start(enc_in, lambda h: enc_in.at[:, pl.ds(32 * h, 32)], e_half, e_whole)

    wa[y, z] = wa_in[...]
    wb[z, y] = wb_in[...]
    fg[j] = f_in[...]
    eg[pl.ds(3 * j, 3)] = enc_in[...]
    dg[pl.ds(3 * j, 3)] = dec_in[...]
    nzg[j] = nz_in[...]
    cg[j] = code_in[...]
    ig[j] = ids_in[...]

    for step in (2, 3, 4):
        arrive(ra)
        ra = a1(step)
        arrive(rb)
        rb = b1(step)
    fx = along_x_forward(fx, f_half, f_whole)
    arrive(ra)
    ra = a2(1)
    arrive(rb)
    rb = b2(1)
    fx = along_x_last(fx, f_half, f_whole)
    arrive(small)
    table = pltpu.make_async_copy(ig, ids, local_sem)
    table.start()
    table.wait()
    arrive(fx)

    def kv_part(b):
        return mm(fg[b][:, : 8 * KA], wa[b].reshape(8 * KA, 2 * HC))

    kv[...] = kv_part(y)
    for step in (2, 3, 4):
        arrive(ra)
        ra = a2(step)
        arrive(rb)
        rb = b2(step)
        kv[...] += kv_part((y - fwd * (step - 1) + 16) % 8)
        kv[...] += kv_part((y + fwd * (step - 1) + 16) % 8)
        if step == 2:
            ex = along_x_forward(ex, e_half, e_whole)
            dx = along_x_start(dec_in, lambda h: dec_in.at[:, pl.ds(32 * h, 32)], d_half, d_whole)
        if step == 3:
            ex = along_x_last(ex, e_half, e_whole)
    arrive(ra)
    arrive(rb)
    kv[...] += kv_part((y + 4) % 8)
    for b in range(8):
        kv[...] += mm(fg[b][:, 8 * KA :], wb[:, b, 0:16, :].reshape(128, 2 * HC))

    def unpack(zz, carry):
        for yy in range(NY):
            qo[yy * NZ + zz] = wb[zz, yy, 16:40, :].astype(F32)
        return carry

    lax.fori_loop(0, NZ, unpack, 0)

    def split(b, carry):
        rows = qo[pl.ds(8 * b, 8)].reshape(HC, 2 * HC)
        wq[pl.ds(pl.multiple_of(HC * b, HC), HC), :] = rows[:, :HC].astype(BF)
        wo[pl.ds(pl.multiple_of(HC * b, HC), HC), :] = rows[:, HC:].astype(BF)
        return carry

    lax.fori_loop(0, NY, split, 0)

    head_of_row = lax.broadcasted_iota(jnp.int32, (32, HC), 0) >> 3
    column = lax.broadcasted_iota(jnp.int32, (32, HC), 1)
    low = head_of_row * HD
    head_mask = jnp.where((column >= low) & (column < low + HD), 1.0, 0.0).astype(F32)

    def spread(flat):
        three = flat.astype(BF).astype(F32).reshape(GROUP, CTX, HC)
        return (jnp.concatenate([three] * 4, axis=1) * head_mask[None]).astype(BF)

    kb[...] = spread(kv[:, :HC])
    vb[...] = spread(kv[:, HC:])

    same_head = jnp.where(
        (lax.broadcasted_iota(jnp.int32, (32, 32), 0) >> 3)
        == (lax.broadcasted_iota(jnp.int32, (32, 32), 1) >> 3), 1.0, 0.0,
    ).astype(F32)

    def head_sum(values):
        return jnp.dot(values, same_head, precision=lax.Precision.HIGHEST, preferred_element_type=F32)

    arrive(ex)
    dx = along_x_forward(dx, d_half, d_whole)
    lane = lax.broadcasted_iota(jnp.int32, (STEPS, 2 * STEPS), 1)
    scale = 1.0 / math.sqrt(HD)

    def two_spans(pair):
        zero = jnp.zeros_like(pair)
        return jnp.concatenate([jnp.where(lane < STEPS, pair, zero), jnp.where(lane >= STEPS, pair, zero)], axis=0)

    def weights_of(buf, p):
        return jnp.concatenate([buf[ids[p, 0, 0]], buf[ids[p, 0, 1]]], axis=0)

    def encode(p, carry):
        enc = mm(two_spans(nzg[p]), weights_of(eg, p)).astype(BF).astype(F32)
        code = cg[p]
        for q in range(2):
            row = jnp.concatenate([code[4 * q + r : 4 * q + r + 1] for r in range(4)], axis=1)
            hid[pl.ds(pl.multiple_of(p * 128 + 64 * q, 64), 64), :] = (enc[64 * q : 64 * q + 64] + row).astype(BF)
        return carry

    lax.fori_loop(0, ne, encode, 0)

    def attend(g, carry):
        here = pl.ds(pl.multiple_of(256 * g, 256), 256)
        queries = mm(hid[here, :], wq[...]).astype(BF)
        scores = jnp.concatenate([mm_nt(queries[64 * s : 64 * s + 64], kb[4 * g + s]) for s in range(4)], axis=0) * scale
        raised = jnp.exp(scores)
        probs = raised / head_sum(raised)
        prs[here, :] = probs
        rounded = probs.astype(BF)
        out = jnp.concatenate([mm(rounded[64 * s : 64 * s + 64], vb[4 * g + s]) for s in range(4)], axis=0)
        att[here, :] = out.astype(BF)
        att_t[:, here] = out.T.astype(BF)
        return carry

    lax.fori_loop(0, 4, attend, 0)
    dx = along_x_last(dx, d_half, d_whole)
    arrive(dx)

    def decode(p, carry):
        here = pl.ds(pl.multiple_of(128 * p, 128), 128)
        own = jnp.where(p == j, 1.0, 0.0).astype(F32)
        branch = (mm_nt(att[here, :], wo[...]) + own * hid[here, :].astype(F32)).astype(BF)
        ps[p] = jnp.concatenate(
            [mm_nt(branch[64 * q : 64 * q + 64], dg[ids[p, 0, q]]) for q in range(2)], axis=1
        ).astype(BF)
        return carry

    lax.fori_loop(0, ne, decode, 0)

    shares = [go(ps.at[(j + k) % ne], pr.at[k - 1], dev_e((j + k) % ne)) for k in range(1, ne)]
    arrive(shares)
    predicted = ps[j].astype(F32)
    for k in range(1, ne):
        predicted += pr[k - 1].astype(F32)
    length, dims = meta_in[0:1, :], meta_in[1:2, :]
    step_row = lax.broadcasted_iota(jnp.int32, (STEPS, 2 * STEPS), 0).astype(F32)
    step_col = (lane & (STEPS - 1)).astype(F32)
    valid = jnp.where((step_row < length) & (step_col < dims), 1.0, 0.0).astype(F32)
    error = predicted - vel_in[...]
    squares = jnp.sum(valid * error * error, axis=0, keepdims=True)
    low_lane = lane[0:1] < STEPS
    for q in range(2):
        one = jnp.sum(jnp.where(low_lane == (q == 0), squares, 0.0), axis=1, keepdims=True)
        loss_out[q : q + 1, :] = one / length[:, 64 * q : 64 * q + 1] + jnp.zeros((1, 128), F32)
    dp_own[...] = (2.0 * valid * error / length).astype(BF)
    errors = [go(dp_own, dpg.at[j], dev_e((j + k) % ne)) for k in range(1, ne)]
    dpg[j] = dp_own[...]
    arrive(errors)

    def d_branch(p, carry):
        here = pl.ds(pl.multiple_of(128 * p, 128), 128)
        dbr[here, :] = mm(two_spans(dpg[p]), weights_of(dg, p)).astype(BF)
        return carry

    lax.fori_loop(0, ne, d_branch, 0)

    def slice_of(left_t, right_rows, t):
        rows = pl.ds(pl.multiple_of(96 * (t // 4), 16), 96)
        columns = pl.ds(pl.multiple_of(384 * (t % 4), 128), 384)
        return mm(left_t[rows, :], right_rows[:, columns])

    def scatter(n, left_t, right_rows, me, device):
        out = []
        for k in range(1, 8):
            t = (me + k) % 8
            gs[n, k - 1] = slice_of(left_t, right_rows, t).astype(BF)
            out.append(go(gs.at[n, k - 1], gr.at[n, k - 1], device(t)))
        return out

    go_copies = scatter(1, att_t, dbr, z, dev_z)

    def back(g, carry):
        here = pl.ds(pl.multiple_of(256 * g, 256), 256)
        d_att = mm(dbr[here, :], wo[...]).astype(BF)
        d_probs = jnp.concatenate([mm_nt(d_att[64 * s : 64 * s + 64], vb[4 * g + s]) for s in range(4)], axis=0)
        probs = prs[here, :]
        d_scores = (probs * (d_probs - head_sum(probs * d_probs))).astype(BF)
        out = jnp.concatenate([mm(d_scores[64 * s : 64 * s + 64], kb[4 * g + s]) for s in range(4)], axis=0) * scale
        dq_t[:, here] = out.T.astype(BF)
        return carry

    lax.fori_loop(0, 4, back, 0)
    gq_copies = scatter(0, dq_t, hid, y, dev_y)

    def add_up(n, copies, left_t, right_rows, me, me2, device2):
        total = slice_of(left_t, right_rows, me)
        arrive(copies)
        for k in range(7):
            total += gr[n, k].astype(F32)
        sb[n, 0:96] = total.astype(BF)
        sb[n, 96:128] = jnp.zeros((32, 384), BF)
        out = []
        for k in range(1, 8):
            t = (me2 + k) % 8
            out.append(go(sb.at[n, pl.ds(pl.multiple_of(16 * t, 16), 16)], sr.at[n, k - 1], device2(t)))
        return out

    def finish(n, copies, me2, device2):
        arrive(copies)
        total = sb[n, pl.ds(pl.multiple_of(16 * me2, 16), 16)].astype(F32)
        for k in range(7):
            total += sr[n, k].astype(F32)
        fs[n] = total.astype(BF)
        out = [go(fs.at[n], sg.at[n, me2], device2((me2 + k) % 8)) for k in range(1, 8)]
        sg[n, me2] = fs[n]
        return out

    def gather(n, copies, me, device):
        arrive(copies)
        out = [go(sg.at[n, pl.ds(0, 6)], og.at[n, me], device((me + k) % 8)) for k in range(1, 8)]
        og[n, me] = sg[n, 0:6]
        return out

    go_copies = add_up(1, go_copies, att_t, dbr, z, y, dev_y)
    gq_copies = add_up(0, gq_copies, dq_t, hid, y, z, dev_z)
    go_copies = finish(1, go_copies, y, dev_y)
    gq_copies = finish(0, gq_copies, z, dev_z)
    go_copies = gather(1, go_copies, z, dev_z)
    gq_copies = gather(0, gq_copies, y, dev_y)
    arrive(go_copies)
    go_out[...] = og[1].reshape(8, 96, 384)
    arrive(gq_copies)
    gq_out[...] = og[0].reshape(8, 96, 384)
    for copy in cs.made:
        copy.wait_send()


def step_embedding(step_values, width):
    half = width // 2
    freq = jnp.exp(-math.log(10000.0) * jnp.arange(half, dtype=F32) / half)
    angle = step_values.astype(F32)[:, None] * freq[None, :]
    return jnp.concatenate([jnp.sin(angle), jnp.cos(angle)], axis=1)


def side_by_side(spans):
    return jnp.concatenate([spans[0], spans[1]], axis=1)


def body(actions, noise, emb_ids, lengths, t_index, act_dims, features, enc_w, dec_w, wq, wk, wv, wo_t):
    shard = jnp.concatenate(
        [jnp.concatenate([wk, wv], axis=1), jnp.concatenate([wq, wo_t], axis=1), jnp.zeros((8, 2 * HC), BF)], axis=0
    )
    flat = features.reshape(GROUP * CTX, 8, 80)
    feats = jnp.concatenate(
        [flat[:, :, :KA].reshape(GROUP * CTX, 8 * KA), flat[:, :, KA:].reshape(GROUP * CTX, 128)], axis=1
    )
    act, noi = actions.astype(F32), noise.astype(F32)
    fraction = (t_index.astype(F32) / TSTEPS)[:, None, None]
    noisy = side_by_side(((1.0 - fraction) * noi + fraction * act).astype(BF))
    velocity = side_by_side(act - noi)
    code = step_embedding(t_index, H).reshape(8, 384)
    dims = act_dims[emb_ids]
    meta = jnp.stack(
        [jnp.repeat(lengths, STEPS).astype(F32), jnp.repeat(dims, STEPS).astype(F32)] + [jnp.ones((128,), F32)] * 6
    )
    ids = jnp.zeros((8, 128), jnp.int32).at[0, 0:2].set(emb_ids)
    vm = pl.BlockSpec(memory_space=pltpu.VMEM)
    V = pltpu.VMEM
    d_q, d_o, loss = pl.pallas_call(
        kernel,
        out_shape=(
            jax.ShapeDtypeStruct((8, 96, 384), BF),
            jax.ShapeDtypeStruct((8, 96, 384), BF),
            jax.ShapeDtypeStruct((8, 128), F32),
        ),
        in_specs=[vm] * 10,
        out_specs=(vm, vm, vm),
        scratch_shapes=[
            V((NY, NZ, KA, 2 * HC), BF),
            V((NZ, NY, KB, 2 * HC), BF),
            V((8, GROUP * CTX, 640), BF),
            V((EMBS, STEPS, H), BF),
            V((EMBS, STEPS, H), BF),
            V((8, STEPS, 128), BF),
            V((8, 8, 384), F32),
            V((8, 8, 128), jnp.int32),
            pltpu.SMEM((8, 8, 128), jnp.int32),
            V((GROUP * CTX, 2 * HC), F32),
            V((64, 24, 2 * HC), F32),
            V((H, HC), BF),
            V((H, HC), BF),
            V((GROUP, 32, HC), BF),
            V((GROUP, 32, HC), BF),
            V((ROWS, H), BF),
            V((ROWS, H), BF),
            V((ROWS, 32), F32),
            V((ROWS, HC), BF),
            V((HC, ROWS), BF),
            V((HC, ROWS), BF),
            V((8, STEPS, 128), BF),
            V((7, STEPS, 128), BF),
            V((STEPS, 128), BF),
            V((8, STEPS, 128), BF),
            V((2, 7, 96, 384), BF),
            V((2, 7, 96, 384), BF),
            V((2, 128, 384), BF),
            V((2, 7, 16, 384), BF),
            V((2, 16, 384), BF),
            V((2, 8, 16, 384), BF),
            V((2, 8, 6, 16, 384), BF),
            pltpu.SemaphoreType.DMA((N_COPIES,)),
            pltpu.SemaphoreType.DMA((N_COPIES,)),
            pltpu.SemaphoreType.DMA,
        ],
        compiler_params=pltpu.CompilerParams(
            collective_id=0, has_side_effects=True, vmem_limit_bytes=56 * 1024 * 1024
        ),
    )(shard[:KA], shard[KA:], feats, enc_w, jnp.swapaxes(dec_w, 1, 2), noisy, velocity, meta, code, ids)

    def whole(slices):
        return slices.astype(F32).reshape(2, 4, 96, 384).transpose(0, 2, 1, 3).reshape(HC, H)

    return whole(d_q), whole(d_o), loss[0:2, 0]


def solution(mesh):
    rows = P(("dp", "emb"))
    in_specs = (
        P(("dp", "emb"), None, None), P(("dp", "emb"), None, None), rows, rows, rows, P(),
        P("dp", None, "emb"), P("emb", None, None), P("emb", None, None),
        P("dp", "emb"), P("dp", "emb"), P("dp", "emb"), P("dp", "emb"),
    )
    out_specs = (P("emb", None), P("emb", None), rows)
    return jax.shard_map(body, mesh=mesh, in_specs=in_specs, out_specs=out_specs, check_vma=False)
```

```python
import functools
import math

import jax
import jax.numpy as jnp
from jax import lax
from jax.experimental import pallas as pl
from jax.experimental.pallas import tpu as pltpu
from jax.sharding import PartitionSpec as P

HD = 48
TSTEPS = 1000
H = 1536
HC = 192
STEPS = 64
EMBS = 24
NY = 8
NZ = 8
NX = 4
GROUP = 16
CTX = 8
ROWS = GROUP * STEPS
RK = 80
RB = 160
MESH = pl.DeviceIdType.MESH
BF = jnp.bfloat16
F32 = jnp.float32
NT = (((1,), (1,)), ((), ()))


def mm(a, b):
    return jnp.dot(a, b, preferred_element_type=F32)


def mm_nt(a, b):
    return lax.dot_general(a, b, NT, preferred_element_type=F32)


class Copies:
    def __init__(self, send, recv):
        self.send, self.recv, self.count, self.made = send, recv, 0, []

    def make(self, src, dst, device):
        k = self.count
        self.count += 1
        copy = pltpu.make_async_remote_copy(
            src_ref=src, dst_ref=dst, send_sem=self.send.at[k], recv_sem=self.recv.at[k],
            device_id=device, device_id_type=MESH,
        )
        copy.start()
        self.made.append(copy)
        return copy


N_COPIES = 256


def kernel(
    act, noise, emb_ids, lengths, levels, act_dims, f_in, enc_in, dec_in, wq_own, wk_own, wv_own, wo_own,
    gq_out, go_out, loss_out,
    wa_in, wb_in, nz_in, vel_in, code_in, ids_in,
    wa, wb, fg, eg, dg, nzg, cg, ig, ids, kv, qo, wq, wo, kb, vb,
    hid, dbr, prs, att, att_t, dq_t, ps, pr, dp_own, dpg,
    gs, gr, sb, sr, fs, sg, og, send_sems, recv_sems, local_sem,
):
    i = lax.axis_index("dp")
    j = lax.axis_index("emb")
    y, z = i // NZ, i % NZ
    x, c = j // 2, j % 2
    ne = 2 * NX

    barrier = pltpu.get_barrier_semaphore()
    for k in range(1, ne):
        pl.semaphore_signal(barrier, inc=1, device_id=(i, (j + k) % ne), device_id_type=MESH)
    for k in range(1, NY):
        pl.semaphore_signal(barrier, inc=1, device_id=(((y + k) % NY) * NZ + z, j), device_id_type=MESH)
    for k in range(1, NZ):
        pl.semaphore_signal(barrier, inc=1, device_id=(y * NZ + (z + k) % NZ, j), device_id_type=MESH)

    wa_in[...] = jnp.concatenate([wk_own[...], wv_own[:, :STEPS]], axis=1)
    wb_in[0:RK, :] = wv_own[:, STEPS:]
    q_own, o_own = wq_own[...].astype(F32), wo_own[...].astype(F32)
    wb_in[RK:RB, :] = jnp.concatenate(
        [q_own[:, :128], jnp.concatenate([q_own[:, 128:], o_own[:, 128:]], axis=1), o_own[:, :128],
         jnp.zeros((8, 128), F32)], axis=0,
    ).astype(BF)
    lane = lax.broadcasted_iota(jnp.int32, (STEPS, 2 * STEPS), 1)
    mixed = []
    for q in range(2):
        fraction = jnp.full((STEPS, STEPS), levels[q].astype(F32), F32) / TSTEPS
        mixed.append((1.0 - fraction) * noise[q].astype(F32) + fraction * act[q].astype(F32))
    nz_in[...] = jnp.concatenate(mixed, axis=1).astype(BF)
    vel_in[...] = jnp.concatenate([act[q].astype(F32) - noise[q].astype(F32) for q in range(2)], axis=1)
    code_row = lax.broadcasted_iota(jnp.int32, (8, 384), 0)
    code_lane = lax.broadcasted_iota(jnp.int32, (8, 384), 1)
    half = H // 2
    freq = jnp.exp(-math.log(10000.0) * (code_lane + 384 * (code_row & 1)).astype(F32) / half)
    level = jnp.where(code_row < 4, levels[0].astype(F32), levels[1].astype(F32))
    angle = level * freq
    code_in[...] = jnp.where((code_row & 2) == 0, jnp.sin(angle), jnp.cos(angle))
    id_lane = lax.broadcasted_iota(jnp.int32, (8, 128), 1)
    ids_in[...] = jnp.where(id_lane == 0, emb_ids[0], emb_ids[1])

    pl.semaphore_wait(barrier, (ne - 1) + (NY - 1) + (NZ - 1))

    cs = Copies(send_sems, recv_sems)
    go = cs.make
    dev_y = lambda t: (t * NZ + z, j)
    dev_z = lambda t: (y * NZ + t, j)
    dev_e = lambda t: (i, t)
    fwd = 1 - 2 * c

    small = []
    for k in range(1, ne):
        peer = dev_e((j + k) % ne)
        small.append(go(nz_in, nzg.at[j], peer))
        small.append(go(code_in, cg.at[j], peer))
        small.append(go(ids_in, ig.at[j], peer))

    def ring(step, me, device, first, block, heavy, light):
        up = device((me + fwd + 8) % 8)
        down = device((me - fwd + 8) % 8)
        out = []
        if step <= heavy:
            b = (me - fwd * (step - 1) + 16) % 8
            for src, dst in zip(first if step == 1 and first else block(b), block(b)):
                out.append(go(src, dst, up))
        if step <= light:
            b = (me + fwd * (step - 1) + 16) % 8
            for src, dst in zip(first if step == 1 and first else block(b), block(b)):
                out.append(go(src, dst, down))
        return out

    def arrive(copies):
        for copy in copies:
            copy.wait_recv()

    a1 = lambda s: ring(s, z, dev_z, [wa_in], lambda b: [wa.at[y, b]], 4, 3)
    b1 = lambda s: ring(s, y, dev_y, [wb_in], lambda b: [wb.at[z, b]], 4, 3)
    a2 = lambda s: ring(s, y, dev_y, None, lambda b: [wa.at[b, pl.ds(0, 4)], wa.at[b, pl.ds(4, 4)]], 4, 3)
    b2 = lambda s: ring(s, z, dev_z, None, lambda b: [wb.at[b, pl.ds(0, 4)], wb.at[b, pl.ds(4, 4)]], 4, 3)

    right, left = (2 * ((x + 1) % NX) + c), (2 * ((x + 3) % NX) + c)
    opposite, sibling = (2 * ((x + 2) % NX) + c), (2 * x + 1 - c)

    def along_x_start(whole_in, half_in, half, whole):
        r0 = go(half_in(0), half(j, 0), dev_e(right))
        l1 = go(half_in(1), half(j, 1), dev_e(left))
        r1 = go(half_in(1), half(j, 1), dev_e(right))
        l0 = go(half_in(0), half(j, 0), dev_e(left))
        s = go(whole_in, whole(j), dev_e(sibling))
        return r0, l1, r1, l0, s

    def along_x_forward(first, half, whole):
        r0, l1, r1, l0, s = first
        r0.wait_recv()
        f0 = go(half(left, 0), half(left, 0), dev_e(right))
        l1.wait_recv()
        f1 = go(half(right, 1), half(right, 1), dev_e(left))
        r1.wait_recv()
        s0 = go(whole(left), whole(left), dev_e(sibling))
        l0.wait_recv()
        s1 = go(whole(right), whole(right), dev_e(sibling))
        return f0, f1, s0, s1, s

    def along_x_last(second, half, whole):
        f0, f1, s0, s1, s = second
        f0.wait_recv()
        f1.wait_recv()
        s2 = go(whole(opposite), whole(opposite), dev_e(sibling))
        return s, s0, s1, s2

    f_half = lambda b, h: fg.at[b, pl.ds(64 * h, 64)]
    f_whole = lambda b: fg.at[b]
    w3 = lambda buf: (
        (lambda b, h: buf.at[pl.ds(3 * b, 3), pl.ds(32 * h, 32)]),
        (lambda b: buf.at[pl.ds(3 * b, 3)]),
    )
    e_half, e_whole = w3(eg)
    d_half, d_whole = w3(dg)

    ra, rb = a1(1), b1(1)
    fx = along_x_start(f_in, lambda h: f_in.at[pl.ds(64 * h, 64)], f_half, f_whole)
    ex = along_x_start(enc_in, lambda h: enc_in.at[:, pl.ds(32 * h, 32)], e_half, e_whole)

    wa[y, z] = wa_in[...]
    wb[z, y] = wb_in[...]
    fg[j] = f_in[...]
    eg[pl.ds(3 * j, 3)] = enc_in[...]
    dg[pl.ds(3 * j, 3)] = dec_in[...]
    nzg[j] = nz_in[...]
    cg[j] = code_in[...]
    ig[j] = ids_in[...]

    for step in (2, 3, 4):
        arrive(ra)
        ra = a1(step)
        arrive(rb)
        rb = b1(step)
    fx = along_x_forward(fx, f_half, f_whole)
    arrive(ra)
    ra = a2(1)
    arrive(rb)
    rb = b2(1)
    fx = along_x_last(fx, f_half, f_whole)
    arrive(small)
    table = pltpu.make_async_copy(ig, ids, local_sem)
    table.start()
    table.wait()
    arrive(fx)

    def kv_part(b):
        return mm(fg[b], wa[b].reshape(8 * RK, 256))

    kv[:, 0:256] = kv_part(y)
    for step in (2, 3, 4):
        arrive(ra)
        ra = a2(step)
        arrive(rb)
        rb = b2(step)
        kv[:, 0:256] += kv_part((y - fwd * (step - 1) + 16) % 8)
        kv[:, 0:256] += kv_part((y + fwd * (step - 1) + 16) % 8)
        if step == 2:
            ex = along_x_forward(ex, e_half, e_whole)
            dx = along_x_start(dec_in, lambda h: dec_in.at[:, pl.ds(32 * h, 32)], d_half, d_whole)
        if step == 3:
            ex = along_x_last(ex, e_half, e_whole)
    arrive(ra)
    arrive(rb)
    kv[:, 0:256] += kv_part((y + 4) % 8)

    def kv_rest(b, total):
        return total + mm(fg[b], wb[:, b, 0:RK, :].reshape(8 * RK, 128))

    kv[:, 256:384] = lax.fori_loop(0, 8, kv_rest, jnp.zeros((GROUP * CTX, 128), F32))

    def unpack(zz, carry):
        for yy in range(NY):
            tiles = wb[zz, yy, RK:RB, :].astype(F32)
            qo[yy * NZ + zz] = jnp.concatenate([tiles[24 * r : 24 * r + 24] for r in range(3)], axis=1)
        return carry

    lax.fori_loop(0, NZ, unpack, 0)

    def split(b, carry):
        rows = qo[pl.ds(8 * b, 8)].reshape(HC, 2 * HC)
        wq[pl.ds(pl.multiple_of(HC * b, HC), HC), :] = rows[:, :HC].astype(BF)
        wo[pl.ds(pl.multiple_of(HC * b, HC), HC), :] = jnp.concatenate([rows[:, 256:], rows[:, HC:256]], axis=1).astype(BF)
        return carry

    lax.fori_loop(0, NY, split, 0)

    head_of_row = lax.broadcasted_iota(jnp.int32, (32, HC), 0) >> 3
    column = lax.broadcasted_iota(jnp.int32, (32, HC), 1)
    low = head_of_row * HD
    head_mask = jnp.where((column >= low) & (column < low + HD), 1.0, 0.0).astype(F32)

    def spread(flat):
        three = flat.astype(BF).astype(F32).reshape(GROUP, CTX, HC)
        return (jnp.concatenate([three] * 4, axis=1) * head_mask[None]).astype(BF)

    kb[...] = spread(kv[:, :HC])
    vb[...] = spread(kv[:, HC:])

    same_head = jnp.where(
        (lax.broadcasted_iota(jnp.int32, (32, 32), 0) >> 3)
        == (lax.broadcasted_iota(jnp.int32, (32, 32), 1) >> 3), 1.0, 0.0,
    ).astype(F32)

    def head_sum(values):
        return jnp.dot(values, same_head, precision=lax.Precision.HIGHEST, preferred_element_type=F32)

    arrive(ex)
    dx = along_x_forward(dx, d_half, d_whole)
    scale = 1.0 / math.sqrt(HD)

    def two_spans(pair):
        zero = jnp.zeros_like(pair)
        return jnp.concatenate([jnp.where(lane < STEPS, pair, zero), jnp.where(lane >= STEPS, pair, zero)], axis=0)

    def weights_of(buf, p):
        return jnp.concatenate([buf[ids[p, 0, 0]], buf[ids[p, 0, 1]]], axis=0)

    def encode(p, carry):
        enc = mm(two_spans(nzg[p]), weights_of(eg, p)).astype(BF).astype(F32)
        code = cg[p]
        for q in range(2):
            row = jnp.concatenate([code[4 * q + r : 4 * q + r + 1] for r in range(4)], axis=1)
            hid[pl.ds(pl.multiple_of(p * 128 + 64 * q, 64), 64), :] = (enc[64 * q : 64 * q + 64] + row).astype(BF)
        return carry

    lax.fori_loop(0, ne, encode, 0)

    def attend(g, carry):
        here = pl.ds(pl.multiple_of(256 * g, 256), 256)
        queries = mm(hid[here, :], wq[...]).astype(BF)
        scores = jnp.concatenate([mm_nt(queries[64 * s : 64 * s + 64], kb[4 * g + s]) for s in range(4)], axis=0) * scale
        raised = jnp.exp(scores)
        probs = raised / head_sum(raised)
        prs[here, :] = probs
        rounded = probs.astype(BF)
        out = jnp.concatenate([mm(rounded[64 * s : 64 * s + 64], vb[4 * g + s]) for s in range(4)], axis=0)
        att[here, :] = out.astype(BF)
        att_t[:, here] = out.T.astype(BF)
        return carry

    lax.fori_loop(0, 4, attend, 0)
    dx = along_x_last(dx, d_half, d_whole)
    arrive(dx)

    def decode(p, carry):
        here = pl.ds(pl.multiple_of(128 * p, 128), 128)
        own = jnp.where(p == j, 1.0, 0.0).astype(F32)
        branch = (mm_nt(att[here, :], wo[...]) + own * hid[here, :].astype(F32)).astype(BF)
        ps[p] = jnp.concatenate(
            [mm_nt(branch[64 * q : 64 * q + 64], dg[ids[p, 0, q]]) for q in range(2)], axis=1
        ).astype(BF)
        return carry

    lax.fori_loop(0, ne, decode, 0)

    shares = [go(ps.at[(j + k) % ne], pr.at[k - 1], dev_e((j + k) % ne)) for k in range(1, ne)]
    arrive(shares)
    predicted = ps[j].astype(F32)
    for k in range(1, ne):
        predicted += pr[k - 1].astype(F32)
    low_lane = lane[0:1] < STEPS
    length = jnp.where(low_lane, lengths[0].astype(F32), lengths[1].astype(F32))
    dims = jnp.where(low_lane, act_dims[emb_ids[0]].astype(F32), act_dims[emb_ids[1]].astype(F32))
    step_row = lax.broadcasted_iota(jnp.int32, (STEPS, 2 * STEPS), 0).astype(F32)
    step_col = (lane & (STEPS - 1)).astype(F32)
    valid = jnp.where((step_row < length) & (step_col < dims), 1.0, 0.0).astype(F32)
    error = predicted - vel_in[...]
    squares = jnp.sum(valid * error * error, axis=0, keepdims=True)
    sums = [jnp.sum(jnp.where(half_lanes, squares, 0.0), axis=1, keepdims=True) for half_lanes in (low_lane, ~low_lane)]
    one = [sums[q] / jnp.full((1, 1), lengths[q].astype(F32), F32) for q in range(2)]
    loss_out[...] = jnp.where(id_lane == 0, one[0], one[1])
    dp_own[...] = (2.0 * valid * error / length).astype(BF)
    errors = [go(dp_own, dpg.at[j], dev_e((j + k) % ne)) for k in range(1, ne)]
    dpg[j] = dp_own[...]
    arrive(errors)

    def d_branch(p, carry):
        here = pl.ds(pl.multiple_of(128 * p, 128), 128)
        dbr[here, :] = mm(two_spans(dpg[p]), weights_of(dg, p)).astype(BF)
        return carry

    lax.fori_loop(0, ne, d_branch, 0)

    def slice_of(left_t, right_rows, t):
        rows = pl.ds(pl.multiple_of(96 * (t // 4), 16), 96)
        columns = pl.ds(pl.multiple_of(384 * (t % 4), 128), 384)
        return mm(left_t[rows, :], right_rows[:, columns])

    def scatter(n, left_t, right_rows, me, device):
        out = []
        for k in range(1, 8):
            t = (me + k) % 8
            gs[n, k - 1] = slice_of(left_t, right_rows, t).astype(BF)
            out.append(go(gs.at[n, k - 1], gr.at[n, k - 1], device(t)))
        return out

    go_copies = scatter(1, att_t, dbr, z, dev_z)

    def back(g, carry):
        here = pl.ds(pl.multiple_of(256 * g, 256), 256)
        d_att = mm(dbr[here, :], wo[...]).astype(BF)
        d_probs = jnp.concatenate([mm_nt(d_att[64 * s : 64 * s + 64], vb[4 * g + s]) for s in range(4)], axis=0)
        probs = prs[here, :]
        d_scores = (probs * (d_probs - head_sum(probs * d_probs))).astype(BF)
        out = jnp.concatenate([mm(d_scores[64 * s : 64 * s + 64], kb[4 * g + s]) for s in range(4)], axis=0) * scale
        dq_t[:, here] = out.T.astype(BF)
        return carry

    lax.fori_loop(0, 4, back, 0)
    gq_copies = scatter(0, dq_t, hid, y, dev_y)

    def add_up(n, copies, left_t, right_rows, me, me2, device2):
        total = slice_of(left_t, right_rows, me)
        arrive(copies)
        for k in range(7):
            total += gr[n, k].astype(F32)
        sb[n, 0:96] = total.astype(BF)
        sb[n, 96:128] = jnp.zeros((32, 384), BF)
        out = []
        for k in range(1, 8):
            t = (me2 + k) % 8
            out.append(go(sb.at[n, pl.ds(pl.multiple_of(16 * t, 16), 16)], sr.at[n, k - 1], device2(t)))
        return out

    def finish(n, copies, me2, device2):
        arrive(copies)
        total = sb[n, pl.ds(pl.multiple_of(16 * me2, 16), 16)].astype(F32)
        for k in range(7):
            total += sr[n, k].astype(F32)
        fs[n] = total.astype(BF)
        out = [go(fs.at[n], sg.at[n, me2], device2((me2 + k) % 8)) for k in range(1, 8)]
        sg[n, me2] = fs[n]
        return out

    def gather(n, copies, me, device):
        arrive(copies)
        out = [go(sg.at[n, pl.ds(0, 6)], og.at[n, me], device((me + k) % 8)) for k in range(1, 8)]
        og[n, me] = sg[n, 0:6]
        return out

    go_copies = add_up(1, go_copies, att_t, dbr, z, y, dev_y)
    gq_copies = add_up(0, gq_copies, dq_t, hid, y, z, dev_z)
    go_copies = finish(1, go_copies, y, dev_y)
    gq_copies = finish(0, gq_copies, z, dev_z)
    go_copies = gather(1, go_copies, z, dev_z)
    gq_copies = gather(0, gq_copies, y, dev_y)
    for n, copies, out in ((1, go_copies, go_out), (0, gq_copies, gq_out)):
        arrive(copies)
        for t in range(8):
            rows, columns = 96 * (t // 4), 384 * (t % 4)
            out[rows : rows + 96, columns : columns + 384] = og[n, t].reshape(96, 384)
    for copy in cs.made:
        copy.wait_send()


def body(actions, noise, emb_ids, lengths, t_index, act_dims, features, enc_w, dec_w, wq, wk, wv, wo_t):
    vm = pl.BlockSpec(memory_space=pltpu.VMEM)
    sm = pl.BlockSpec(memory_space=pltpu.SMEM)
    V = pltpu.VMEM
    d_q, d_o, loss = pl.pallas_call(
        kernel,
        out_shape=(
            jax.ShapeDtypeStruct((HC, H), BF),
            jax.ShapeDtypeStruct((HC, H), BF),
            jax.ShapeDtypeStruct((8, 128), F32),
        ),
        in_specs=[vm] * 2 + [sm] * 4 + [vm] * 7,
        out_specs=(vm, vm, vm),
        scratch_shapes=[
            V((RK, 256), BF),
            V((RB, 128), BF),
            V((STEPS, 128), BF),
            V((STEPS, 128), F32),
            V((8, 384), F32),
            V((8, 128), jnp.int32),
            V((NY, NZ, RK, 256), BF),
            V((NZ, NY, RB, 128), BF),
            V((8, GROUP * CTX, 640), BF),
            V((EMBS, STEPS, H), BF),
            V((EMBS, STEPS, H), BF),
            V((8, STEPS, 128), BF),
            V((8, 8, 384), F32),
            V((8, 8, 128), jnp.int32),
            pltpu.SMEM((8, 8, 128), jnp.int32),
            V((GROUP * CTX, 2 * HC), F32),
            V((64, 24, 2 * HC), F32),
            V((H, HC), BF),
            V((H, HC), BF),
            V((GROUP, 32, HC), BF),
            V((GROUP, 32, HC), BF),
            V((ROWS, H), BF),
            V((ROWS, H), BF),
            V((ROWS, 32), F32),
            V((ROWS, HC), BF),
            V((HC, ROWS), BF),
            V((HC, ROWS), BF),
            V((8, STEPS, 128), BF),
            V((7, STEPS, 128), BF),
            V((STEPS, 128), BF),
            V((8, STEPS, 128), BF),
            V((2, 7, 96, 384), BF),
            V((2, 7, 96, 384), BF),
            V((2, 128, 384), BF),
            V((2, 7, 16, 384), BF),
            V((2, 16, 384), BF),
            V((2, 8, 16, 384), BF),
            V((2, 8, 6, 16, 384), BF),
            pltpu.SemaphoreType.DMA((N_COPIES,)),
            pltpu.SemaphoreType.DMA((N_COPIES,)),
            pltpu.SemaphoreType.DMA,
        ],
        compiler_params=pltpu.CompilerParams(
            collective_id=0, has_side_effects=True, vmem_limit_bytes=56 * 1024 * 1024
        ),
    )(
        actions, noise, emb_ids, lengths, t_index, act_dims, features.reshape(GROUP * CTX, 640), enc_w,
        jnp.swapaxes(dec_w, 1, 2), wq, wk, wv, wo_t,
    )
    return d_q.astype(F32), d_o.astype(F32), loss[0, 0:2]


def solution(mesh):
    rows = P(("dp", "emb"))
    in_specs = (
        P(("dp", "emb"), None, None), P(("dp", "emb"), None, None), rows, rows, rows, P(),
        P("dp", None, "emb"), P("emb", None, None), P("emb", None, None),
        P("dp", "emb"), P("dp", "emb"), P("dp", "emb"), P("dp", "emb"),
    )
    out_specs = (P("emb", None), P("emb", None), rows)
    return jax.shard_map(body, mesh=mesh, in_specs=in_specs, out_specs=out_specs, check_vma=False)
```

```python
import functools
import math

import jax
import jax.numpy as jnp
from jax import lax
from jax.experimental import pallas as pl
from jax.experimental.pallas import tpu as pltpu
from jax.sharding import PartitionSpec as P

HD = 48
TSTEPS = 1000
H = 1536
HC = 192
STEPS = 64
EMBS = 24
NY = 8
NZ = 8
NX = 4
GROUP = 16
CTX = 8
ROWS = GROUP * STEPS
RK = 80
RB = 160
MESH = pl.DeviceIdType.MESH
BF = jnp.bfloat16
F32 = jnp.float32
NT = (((1,), (1,)), ((), ()))


def mm(a, b):
    return jnp.dot(a, b, preferred_element_type=F32)


def mm_nt(a, b):
    return lax.dot_general(a, b, NT, preferred_element_type=F32)


class Copies:
    def __init__(self, send, recv):
        self.send, self.recv, self.count, self.made = send, recv, 0, []

    def make(self, src, dst, device):
        k = self.count
        self.count += 1
        copy = pltpu.make_async_remote_copy(
            src_ref=src, dst_ref=dst, send_sem=self.send.at[k], recv_sem=self.recv.at[k],
            device_id=device, device_id_type=MESH,
        )
        copy.start()
        self.made.append(copy)
        return copy


N_COPIES = 256


def kernel(
    act, noise, emb_ids, lengths, levels, act_dims, f_in, enc_in, dec_in, wq_own, wk_own, wv_own, wo_own,
    gq_out, go_out, loss_out,
    wa_in, wb_in, nz_in, vel_in, code_in, ids_in,
    wa, wb, fg, eg, dg, nzg, cg, ig, ids, kv, qo, wq, wo, kb, vb,
    hid, dbr, prs, att, att_t, dq_t, ps, pr, dp_own, dpg,
    gs, own_slice, gr, sb, sr, fs, sg, og, send_sems, recv_sems, local_sem,
):
    i = lax.axis_index("dp")
    j = lax.axis_index("emb")
    y, z = i // NZ, i % NZ
    x, c = j // 2, j % 2
    ne = 2 * NX

    barrier = pltpu.get_barrier_semaphore()
    for k in range(1, ne):
        pl.semaphore_signal(barrier, inc=1, device_id=(i, (j + k) % ne), device_id_type=MESH)
    for k in range(1, NY):
        pl.semaphore_signal(barrier, inc=1, device_id=(((y + k) % NY) * NZ + z, j), device_id_type=MESH)
    for k in range(1, NZ):
        pl.semaphore_signal(barrier, inc=1, device_id=(y * NZ + (z + k) % NZ, j), device_id_type=MESH)

    wa_in[...] = jnp.concatenate([wk_own[...], wv_own[:, :STEPS]], axis=1)
    wb_in[0:RK, :] = wv_own[:, STEPS:]
    q_own, o_own = wq_own[...].astype(F32), wo_own[...].astype(F32)
    wb_in[RK:RB, :] = jnp.concatenate(
        [q_own[:, :128], jnp.concatenate([q_own[:, 128:], o_own[:, 128:]], axis=1), o_own[:, :128],
         jnp.zeros((8, 128), F32)], axis=0,
    ).astype(BF)
    lane = lax.broadcasted_iota(jnp.int32, (STEPS, 2 * STEPS), 1)
    mixed = []
    for q in range(2):
        fraction = jnp.full((STEPS, STEPS), levels[q].astype(F32), F32) / TSTEPS
        mixed.append((1.0 - fraction) * noise[q].astype(F32) + fraction * act[q].astype(F32))
    nz_in[...] = jnp.concatenate(mixed, axis=1).astype(BF)
    vel_in[...] = jnp.concatenate([act[q].astype(F32) - noise[q].astype(F32) for q in range(2)], axis=1)
    code_row = lax.broadcasted_iota(jnp.int32, (8, 384), 0)
    code_lane = lax.broadcasted_iota(jnp.int32, (8, 384), 1)
    half = H // 2
    freq = jnp.exp(-math.log(10000.0) * (code_lane + 384 * (code_row & 1)).astype(F32) / half)
    level = jnp.where(code_row < 4, levels[0].astype(F32), levels[1].astype(F32))
    angle = level * freq
    code_in[...] = jnp.where((code_row & 2) == 0, jnp.sin(angle), jnp.cos(angle))
    id_lane = lax.broadcasted_iota(jnp.int32, (8, 128), 1)
    ids_in[...] = jnp.where(id_lane == 0, emb_ids[0], emb_ids[1])

    pl.semaphore_wait(barrier, (ne - 1) + (NY - 1) + (NZ - 1))

    cs = Copies(send_sems, recv_sems)
    go = cs.make
    dev_y = lambda t: (t * NZ + z, j)
    dev_z = lambda t: (y * NZ + t, j)
    dev_e = lambda t: (i, t)
    fwd = 1 - 2 * c

    small = []
    for k in range(1, ne):
        peer = dev_e((j + k) % ne)
        small.append(go(nz_in, nzg.at[j], peer))
        small.append(go(code_in, cg.at[j], peer))
        small.append(go(ids_in, ig.at[j], peer))

    def arrive(copies):
        for copy in copies:
            copy.wait_recv()

    def first_ring(step, me, device, own, slot):
        out = [go(own if step == 1 else slot(2 * step - 3), slot(2 * step - 1), device((me + fwd + 8) % 8))]
        if step <= 3:
            out.append(go(own if step == 1 else slot(2 * step - 2), slot(2 * step), device((me - fwd + 8) % 8)))
        return out

    pieces = ((0, 3), (3, 2), (5, 3))

    def second_ring(step, piece, me, device, buf):
        start, size = pieces[piece]
        b = (me - fwd * (step - 1) + 16) % 8
        block = buf.at[b, pl.ds(start, size)]
        out = [go(block, block, device((me + fwd + 8) % 8))]
        if step <= 3:
            b = (me + fwd * (step - 1) + 16) % 8
            block = buf.at[b, pl.ds(start, size)]
            out.append(go(block, block, device((me - fwd + 8) % 8)))
        return out

    def place_of(t, me):
        away = ((t - me) * fwd + 8) % 8
        return 2 * away - (away // 4) * (4 * away - 15)

    a1 = lambda s: first_ring(s, z, dev_z, wa_in, lambda p: wa.at[y, p])
    b1 = lambda s: first_ring(s, y, dev_y, wb_in, lambda p: wb.at[z, p])
    a2 = lambda s, p: second_ring(s, p, y, dev_y, wa)
    b2 = lambda s, p: second_ring(s, p, z, dev_z, wb)

    right, left = (2 * ((x + 1) % NX) + c), (2 * ((x + 3) % NX) + c)
    opposite, sibling = (2 * ((x + 2) % NX) + c), (2 * x + 1 - c)

    def along_x_start(whole_in, half_in, half, whole):
        r0 = go(half_in(0), half(j, 0), dev_e(right))
        l1 = go(half_in(1), half(j, 1), dev_e(left))
        r1 = go(half_in(1), half(j, 1), dev_e(right))
        l0 = go(half_in(0), half(j, 0), dev_e(left))
        s = go(whole_in, whole(j), dev_e(sibling))
        return r0, l1, r1, l0, s

    def along_x_forward(first, half, whole):
        r0, l1, r1, l0, s = first
        r0.wait_recv()
        f0 = go(half(left, 0), half(left, 0), dev_e(right))
        l1.wait_recv()
        f1 = go(half(right, 1), half(right, 1), dev_e(left))
        r1.wait_recv()
        s0 = go(whole(left), whole(left), dev_e(sibling))
        l0.wait_recv()
        s1 = go(whole(right), whole(right), dev_e(sibling))
        return f0, f1, s0, s1, s

    def along_x_last(second, half, whole):
        f0, f1, s0, s1, s = second
        f0.wait_recv()
        f1.wait_recv()
        s2 = go(whole(opposite), whole(opposite), dev_e(sibling))
        return s, s0, s1, s2

    f_half = lambda b, h: fg.at[b, pl.ds(64 * h, 64)]
    f_whole = lambda b: fg.at[b]
    w3 = lambda buf: (
        (lambda b, h: buf.at[pl.ds(3 * b, 3), pl.ds(32 * h, 32)]),
        (lambda b: buf.at[pl.ds(3 * b, 3)]),
    )
    e_half, e_whole = w3(eg)
    d_half, d_whole = w3(dg)

    ra, rb = a1(1), b1(1)
    fx = along_x_start(f_in, lambda h: f_in.at[pl.ds(64 * h, 64)], f_half, f_whole)
    ex = along_x_start(enc_in, lambda h: enc_in.at[:, pl.ds(32 * h, 32)], e_half, e_whole)

    wa[y, 0] = wa_in[...]
    wb[z, 0] = wb_in[...]
    fg[j] = f_in[...]
    eg[pl.ds(3 * j, 3)] = enc_in[...]
    dg[pl.ds(3 * j, 3)] = dec_in[...]
    nzg[j] = nz_in[...]
    cg[j] = code_in[...]
    ig[j] = ids_in[...]

    ring = []
    for step in (1, 2, 3, 4):
        arrive(ra)
        arrive(rb)
        if step < 4:
            ra, rb = a1(step + 1), b1(step + 1)
        if step != 3:
            piece = len(ring)
            ring.append((a2(1, piece), b2(1, piece)))
    fx = along_x_forward(fx, f_half, f_whole)
    fx = along_x_last(fx, f_half, f_whole)
    arrive(small)
    table = pltpu.make_async_copy(ig, ids, local_sem)
    table.start()
    table.wait()
    arrive(fx)

    def kv_part(b):
        rows = jnp.concatenate([wa[b, place_of(t, z)] for t in range(8)], axis=0)
        return mm(fg[b], rows)

    kv[:, 0:256] = kv_part(y)

    def encode(p, carry):
        enc = mm(two_spans(nzg[p]), weights_of(eg, p)).astype(BF).astype(F32)
        code = cg[p]
        for q in range(2):
            row = jnp.concatenate([code[4 * q + r : 4 * q + r + 1] for r in range(4)], axis=1)
            hid[pl.ds(pl.multiple_of(p * 128 + 64 * q, 64), 64), :] = (enc[64 * q : 64 * q + 64] + row).astype(BF)
        return carry

    def two_spans(pair):
        zero = jnp.zeros_like(pair)
        return jnp.concatenate([jnp.where(lane < STEPS, pair, zero), jnp.where(lane >= STEPS, pair, zero)], axis=0)

    def weights_of(buf, p):
        return jnp.concatenate([buf[ids[p, 0, 0]], buf[ids[p, 0, 1]]], axis=0)

    for step in (2, 3, 4):
        later = []
        for piece in range(3):
            for copies in ring[piece]:
                arrive(copies)
            later.append((a2(step, piece), b2(step, piece)))
        ring = later
        if step == 2:
            ex = along_x_forward(ex, e_half, e_whole)
            dx = along_x_start(dec_in, lambda h: dec_in.at[:, pl.ds(32 * h, 32)], d_half, d_whole)
        if step == 3:
            ex = along_x_last(ex, e_half, e_whole)
        kv[:, 0:256] += kv_part((y - fwd * (step - 1) + 16) % 8)
        kv[:, 0:256] += kv_part((y + fwd * (step - 1) + 16) % 8)
    arrive(ex)
    lax.fori_loop(0, ne, encode, 0)
    for piece in range(3):
        for copies in ring[piece]:
            arrive(copies)
    dx = along_x_forward(dx, d_half, d_whole)
    kv[:, 0:256] += kv_part((y + 4) % 8)

    def kv_rest(b, total):
        return total + mm(fg[b], wb[:, place_of(b, y), 0:RK, :].reshape(8 * RK, 128))

    kv[:, 256:384] = lax.fori_loop(0, 8, kv_rest, jnp.zeros((GROUP * CTX, 128), F32))

    def unpack(zz, carry):
        for yy in range(NY):
            tiles = wb[zz, place_of(yy, y), RK:RB, :].astype(F32)
            qo[yy * NZ + zz] = jnp.concatenate([tiles[24 * r : 24 * r + 24] for r in range(3)], axis=1)
        return carry

    lax.fori_loop(0, NZ, unpack, 0)

    def split(b, carry):
        rows = qo[pl.ds(8 * b, 8)].reshape(HC, 2 * HC)
        wq[pl.ds(pl.multiple_of(HC * b, HC), HC), :] = rows[:, :HC].astype(BF)
        wo[pl.ds(pl.multiple_of(HC * b, HC), HC), :] = jnp.concatenate([rows[:, 256:], rows[:, HC:256]], axis=1).astype(BF)
        return carry

    lax.fori_loop(0, NY, split, 0)

    head_of_row = lax.broadcasted_iota(jnp.int32, (32, HC), 0) >> 3
    column = lax.broadcasted_iota(jnp.int32, (32, HC), 1)
    low = head_of_row * HD
    head_mask = jnp.where((column >= low) & (column < low + HD), 1.0, 0.0).astype(F32)

    def spread(flat):
        three = flat.astype(BF).astype(F32).reshape(GROUP, CTX, HC)
        return (jnp.concatenate([three] * 4, axis=1) * head_mask[None]).astype(BF)

    kb[...] = spread(kv[:, :HC])
    vb[...] = spread(kv[:, HC:])

    same_head = jnp.where(
        (lax.broadcasted_iota(jnp.int32, (32, 32), 0) >> 3)
        == (lax.broadcasted_iota(jnp.int32, (32, 32), 1) >> 3), 1.0, 0.0,
    ).astype(F32)

    def head_sum(values):
        return jnp.dot(values, same_head, precision=lax.Precision.HIGHEST, preferred_element_type=F32)

    scale = 1.0 / math.sqrt(HD)

    def attend(g, carry):
        here = pl.ds(pl.multiple_of(256 * g, 256), 256)
        queries = mm(hid[here, :], wq[...]).astype(BF)
        scores = jnp.concatenate([mm_nt(queries[64 * s : 64 * s + 64], kb[4 * g + s]) for s in range(4)], axis=0) * scale
        raised = jnp.exp(scores)
        probs = raised / head_sum(raised)
        prs[here, :] = probs
        rounded = probs.astype(BF)
        out = jnp.concatenate([mm(rounded[64 * s : 64 * s + 64], vb[4 * g + s]) for s in range(4)], axis=0)
        att[here, :] = out.astype(BF)
        att_t[:, here] = out.T.astype(BF)
        return carry

    lax.fori_loop(0, 4, attend, 0)
    dx = along_x_last(dx, d_half, d_whole)
    arrive(dx)

    def decode(p, carry):
        here = pl.ds(pl.multiple_of(128 * p, 128), 128)
        own = jnp.where(p == j, 1.0, 0.0).astype(F32)
        branch = (mm_nt(att[here, :], wo[...]) + own * hid[here, :].astype(F32)).astype(BF)
        ps[p] = jnp.concatenate(
            [mm_nt(branch[64 * q : 64 * q + 64], dg[ids[p, 0, q]]) for q in range(2)], axis=1
        ).astype(BF)
        return carry

    lax.fori_loop(0, ne, decode, 0)

    shares = [go(ps.at[(j + k) % ne], pr.at[k - 1], dev_e((j + k) % ne)) for k in range(1, ne)]
    arrive(shares)
    predicted = ps[j].astype(F32)
    for k in range(1, ne):
        predicted += pr[k - 1].astype(F32)
    low_lane = lane[0:1] < STEPS
    length = jnp.where(low_lane, lengths[0].astype(F32), lengths[1].astype(F32))
    dims = jnp.where(low_lane, act_dims[emb_ids[0]].astype(F32), act_dims[emb_ids[1]].astype(F32))
    step_row = lax.broadcasted_iota(jnp.int32, (STEPS, 2 * STEPS), 0).astype(F32)
    step_col = (lane & (STEPS - 1)).astype(F32)
    valid = jnp.where((step_row < length) & (step_col < dims), 1.0, 0.0).astype(F32)
    error = predicted - vel_in[...]
    squares = jnp.sum(valid * error * error, axis=0, keepdims=True)
    sums = [jnp.sum(jnp.where(half_lanes, squares, 0.0), axis=1, keepdims=True) for half_lanes in (low_lane, ~low_lane)]
    one = [sums[q] / jnp.full((1, 1), lengths[q].astype(F32), F32) for q in range(2)]
    loss_out[...] = jnp.where(id_lane == 0, one[0], one[1])
    dp_own[...] = (2.0 * valid * error / length).astype(BF)
    errors = [go(dp_own, dpg.at[j], dev_e((j + k) % ne)) for k in range(1, ne)]
    dpg[j] = dp_own[...]
    arrive(errors)

    def d_branch(p, carry):
        here = pl.ds(pl.multiple_of(128 * p, 128), 128)
        dbr[here, :] = mm(two_spans(dpg[p]), weights_of(dg, p)).astype(BF)
        return carry

    lax.fori_loop(0, ne, d_branch, 0)

    first_of = ((y, dev_y), (z, dev_z))

    def scatter(n, left_t, right_rows):
        out = []
        for h, (me, device) in enumerate(first_of):
            for k in (1, 2, 3, 0):
                columns = pl.ds(pl.multiple_of(384 * ((me + k) % 4), 128), 384)
                part = mm(left_t[96 * h : 96 * h + 96, :], right_rows[:, columns])
                gs[n, h, k] = part.astype(BF)
                if k == 0:
                    upper = jnp.where(me // 4 == 0, 1.0, 0.0).astype(F32)
                    own_slice[n, h] = upper * part[0:48] + (1.0 - upper) * part[48:96]
                for o in (k, k + 4):
                    if o:
                        t = (me + o) % 8
                        rows = pl.ds(pl.multiple_of(48 * (t // 4), 16), 48)
                        out.append(go(gs.at[n, h, k, rows], gr.at[n, h, o - 1], device(t)))
        return out

    go_copies = scatter(1, att_t, dbr)

    def back(g, carry):
        here = pl.ds(pl.multiple_of(256 * g, 256), 256)
        d_att = mm(dbr[here, :], wo[...]).astype(BF)
        d_probs = jnp.concatenate([mm_nt(d_att[64 * s : 64 * s + 64], vb[4 * g + s]) for s in range(4)], axis=0)
        probs = prs[here, :]
        d_scores = (probs * (d_probs - head_sum(probs * d_probs))).astype(BF)
        out = jnp.concatenate([mm(d_scores[64 * s : 64 * s + 64], kb[4 * g + s]) for s in range(4)], axis=0) * scale
        dq_t[:, here] = out.T.astype(BF)
        return carry

    lax.fori_loop(0, 4, back, 0)
    gq_copies = scatter(0, dq_t, hid)

    def add_up(n, copies):
        arrive(copies)
        out = []
        for h in range(2):
            total = own_slice[n, h]
            for k in range(7):
                total += gr[n, h, k].astype(F32)
            for t in range(9):
                sb[n, h, t] = total[16 * (t // 3) : 16 * (t // 3) + 16, 128 * (t % 3) : 128 * (t % 3) + 128].astype(BF)
            me, device = first_of[1 - h]
            for k in range(1, 8):
                t = (me + k) % 8
                out.append(go(sb.at[n, h, pl.ds(2 * t, 2)], sr.at[n, h, k - 1], device(t)))
        return out

    def finish(n, copies):
        arrive(copies)
        out = []
        for h in range(2):
            me, device = first_of[1 - h]
            total = sb[n, h, pl.ds(2 * me, 2)].astype(F32)
            for k in range(7):
                total += sr[n, h, k].astype(F32)
            fs[n, h] = total.astype(BF)
            out += [go(fs.at[n, h], sg.at[n, h, pl.ds(2 * me, 2)], device((me + k) % 8)) for k in range(1, 8)]
            sg[n, h, pl.ds(2 * me, 2)] = fs[n, h]
        return out

    def gather(n, step, copies):
        arrive(copies)
        out = []
        for h, (me, device) in enumerate(first_of):
            b = (me - fwd * (step - 1) + 16) % 8
            first = sg.at[n, h, pl.ds(0, 9)]
            out.append(go(first if step == 1 else og.at[n, h, b], og.at[n, h, b], device((me + fwd + 8) % 8)))
            if step <= 3:
                b = (me + fwd * (step - 1) + 16) % 8
                out.append(go(first if step == 1 else og.at[n, h, b], og.at[n, h, b], device((me - fwd + 8) % 8)))
            if step == 1:
                og[n, h, me] = sg[n, h, 0:9]
        return out

    def write(n, out):
        for h in range(2):
            for t in range(8):
                for r in range(9):
                    row, column = 96 * h + 48 * (t // 4) + 16 * (r // 3), 384 * (t % 4) + 128 * (r % 3)
                    out[row : row + 16, column : column + 128] = og[n, h, t, r]

    sb[:, :, 9:16] = jnp.zeros((2, 2, 7, 16, 128), BF)
    go_copies = add_up(1, go_copies)
    go_copies = finish(1, go_copies)
    gq_copies = add_up(0, gq_copies)
    go_copies = gather(1, 1, go_copies)
    gq_copies = finish(0, gq_copies)
    go_copies = gather(1, 2, go_copies)
    gq_copies = gather(0, 1, gq_copies)
    go_copies = gather(1, 3, go_copies)
    gq_copies = gather(0, 2, gq_copies)
    go_copies = gather(1, 4, go_copies)
    gq_copies = gather(0, 3, gq_copies)
    arrive(go_copies)
    gq_copies = gather(0, 4, gq_copies)
    write(1, go_out)
    arrive(gq_copies)
    write(0, gq_out)
    for copy in cs.made:
        copy.wait_send()


def widen(q_in, o_in, loss_in, q_out, o_out, loss_out):
    q_out[...] = q_in[...].astype(F32)
    o_out[...] = o_in[...].astype(F32)
    for q in range(2):
        loss_out[q] = loss_in[0, q]


def body(actions, noise, emb_ids, lengths, t_index, act_dims, features, enc_w, dec_w, wq, wk, wv, wo_t):
    vm = pl.BlockSpec(memory_space=pltpu.VMEM)
    sm = pl.BlockSpec(memory_space=pltpu.SMEM)
    V = pltpu.VMEM
    d_q, d_o, loss = pl.pallas_call(
        kernel,
        out_shape=(
            jax.ShapeDtypeStruct((HC, H), BF),
            jax.ShapeDtypeStruct((HC, H), BF),
            jax.ShapeDtypeStruct((8, 128), F32),
        ),
        in_specs=[vm] * 2 + [sm] * 4 + [vm] * 7,
        out_specs=(vm, vm, vm),
        scratch_shapes=[
            V((RK, 256), BF),
            V((RB, 128), BF),
            V((STEPS, 128), BF),
            V((STEPS, 128), F32),
            V((8, 384), F32),
            V((8, 128), jnp.int32),
            V((NY, NZ, RK, 256), BF),
            V((NZ, NY, RB, 128), BF),
            V((8, GROUP * CTX, 640), BF),
            V((EMBS, STEPS, H), BF),
            V((EMBS, STEPS, H), BF),
            V((8, STEPS, 128), BF),
            V((8, 8, 384), F32),
            V((8, 8, 128), jnp.int32),
            pltpu.SMEM((8, 8, 128), jnp.int32),
            V((GROUP * CTX, 2 * HC), F32),
            V((64, 24, 2 * HC), F32),
            V((H, HC), BF),
            V((H, HC), BF),
            V((GROUP, 32, HC), BF),
            V((GROUP, 32, HC), BF),
            V((ROWS, H), BF),
            V((ROWS, H), BF),
            V((ROWS, 32), F32),
            V((ROWS, HC), BF),
            V((HC, ROWS), BF),
            V((HC, ROWS), BF),
            V((8, STEPS, 128), BF),
            V((7, STEPS, 128), BF),
            V((STEPS, 128), BF),
            V((8, STEPS, 128), BF),
            V((2, 2, 4, 96, 384), BF),
            V((2, 2, 48, 384), F32),
            V((2, 2, 7, 48, 384), BF),
            V((2, 2, 16, 16, 128), BF),
            V((2, 2, 7, 2, 16, 128), BF),
            V((2, 2, 2, 16, 128), BF),
            V((2, 2, 16, 16, 128), BF),
            V((2, 2, 8, 9, 16, 128), BF),
            pltpu.SemaphoreType.DMA((N_COPIES,)),
            pltpu.SemaphoreType.DMA((N_COPIES,)),
            pltpu.SemaphoreType.DMA,
        ],
        compiler_params=pltpu.CompilerParams(
            collective_id=0, has_side_effects=True, vmem_limit_bytes=56 * 1024 * 1024
        ),
    )(
        actions, noise, emb_ids, lengths, t_index, act_dims, features.reshape(GROUP * CTX, 640), enc_w,
        jnp.swapaxes(dec_w, 1, 2), wq, wk, wv, wo_t,
    )
    return pl.pallas_call(
        widen,
        out_shape=(
            jax.ShapeDtypeStruct((HC, H), F32), jax.ShapeDtypeStruct((HC, H), F32), jax.ShapeDtypeStruct((2,), F32),
        ),
        in_specs=[vm, vm, sm],
        out_specs=(vm, vm, sm),
    )(d_q, d_o, loss)


def solution(mesh):
    rows = P(("dp", "emb"))
    in_specs = (
        P(("dp", "emb"), None, None), P(("dp", "emb"), None, None), rows, rows, rows, P(),
        P("dp", None, "emb"), P("emb", None, None), P("emb", None, None),
        P("dp", "emb"), P("dp", "emb"), P("dp", "emb"), P("dp", "emb"),
    )
    out_specs = (P("emb", None), P("emb", None), rows)
    return jax.shard_map(body, mesh=mesh, in_specs=in_specs, out_specs=out_specs, check_vma=False)
```

```python
import functools
import math

import jax
import jax.numpy as jnp
from jax import lax
from jax.experimental import pallas as pl
from jax.experimental.pallas import tpu as pltpu
from jax.sharding import PartitionSpec as P

HD = 48
TSTEPS = 1000
H = 1536
HC = 192
STEPS = 64
EMBS = 24
NY = 8
NZ = 8
NX = 4
GROUP = 16
CTX = 8
ROWS = GROUP * STEPS
RK = 80
RB = 160
MESH = pl.DeviceIdType.MESH
BF = jnp.bfloat16
F32 = jnp.float32
NT = (((1,), (1,)), ((), ()))


def mm(a, b):
    return jnp.dot(a, b, preferred_element_type=F32)


def mm_nt(a, b):
    return lax.dot_general(a, b, NT, preferred_element_type=F32)


class Copies:
    def __init__(self, send, recv):
        self.send, self.recv, self.count, self.made = send, recv, 0, []

    def make(self, src, dst, device):
        k = self.count
        self.count += 1
        copy = pltpu.make_async_remote_copy(
            src_ref=src, dst_ref=dst, send_sem=self.send.at[k], recv_sem=self.recv.at[k],
            device_id=device, device_id_type=MESH,
        )
        copy.start()
        self.made.append(copy)
        return copy


N_COPIES = 256


def kernel(
    act, noise, emb_ids, lengths, levels, act_dims, f_in, enc_in, dec_in, wq_own, wk_own, wv_own, wo_own,
    gq_out, go_out, loss_out,
    wa_in, wb_in, nz_in, vel_in, code_in, ids_in,
    wa, wb, fg, eg, dg, nzg, cg, ig, ids, kv, qo, wq, wo, kb, vb,
    hid, dbr, prs, att, att_t, dq_t, ps, pr, dp_own, dpg,
    gs, wide, own_slice, gr, sb, sr, fs, sg, og, send_sems, recv_sems, local_sem,
):
    i = lax.axis_index("dp")
    j = lax.axis_index("emb")
    y, z = i // NZ, i % NZ
    x, c = j // 2, j % 2
    ne = 2 * NX

    barrier = pltpu.get_barrier_semaphore()
    for k in range(1, ne):
        pl.semaphore_signal(barrier, inc=1, device_id=(i, (j + k) % ne), device_id_type=MESH)
    for k in range(1, NY):
        pl.semaphore_signal(barrier, inc=1, device_id=(((y + k) % NY) * NZ + z, j), device_id_type=MESH)
    for k in range(1, NZ):
        pl.semaphore_signal(barrier, inc=1, device_id=(y * NZ + (z + k) % NZ, j), device_id_type=MESH)

    wa_in[...] = jnp.concatenate([wk_own[...], wv_own[:, :STEPS]], axis=1)
    wb_in[0:RK, :] = wv_own[:, STEPS:]
    q_own, o_own = wq_own[...].astype(F32), wo_own[...].astype(F32)
    wb_in[RK:RB, :] = jnp.concatenate(
        [q_own[:, :128], jnp.concatenate([q_own[:, 128:], o_own[:, 128:]], axis=1), o_own[:, :128],
         jnp.zeros((8, 128), F32)], axis=0,
    ).astype(BF)
    lane = lax.broadcasted_iota(jnp.int32, (STEPS, 2 * STEPS), 1)
    mixed = []
    for q in range(2):
        fraction = jnp.full((STEPS, STEPS), levels[q].astype(F32), F32) / TSTEPS
        mixed.append((1.0 - fraction) * noise[q].astype(F32) + fraction * act[q].astype(F32))
    nz_in[...] = jnp.concatenate(mixed, axis=1).astype(BF)
    vel_in[...] = jnp.concatenate([act[q].astype(F32) - noise[q].astype(F32) for q in range(2)], axis=1)
    code_row = lax.broadcasted_iota(jnp.int32, (8, 384), 0)
    code_lane = lax.broadcasted_iota(jnp.int32, (8, 384), 1)
    half = H // 2
    freq = jnp.exp(-math.log(10000.0) * (code_lane + 384 * (code_row & 1)).astype(F32) / half)
    level = jnp.where(code_row < 4, levels[0].astype(F32), levels[1].astype(F32))
    angle = level * freq
    code_in[...] = jnp.where((code_row & 2) == 0, jnp.sin(angle), jnp.cos(angle))
    id_lane = lax.broadcasted_iota(jnp.int32, (8, 128), 1)
    ids_in[...] = jnp.where(id_lane == 0, emb_ids[0], emb_ids[1])

    pl.semaphore_wait(barrier, (ne - 1) + (NY - 1) + (NZ - 1))

    cs = Copies(send_sems, recv_sems)
    go = cs.make
    dev_y = lambda t: (t * NZ + z, j)
    dev_z = lambda t: (y * NZ + t, j)
    dev_e = lambda t: (i, t)
    fwd = 1 - 2 * c

    small = []
    for k in range(1, ne):
        peer = dev_e((j + k) % ne)
        small.append(go(nz_in, nzg.at[j], peer))
        small.append(go(code_in, cg.at[j], peer))
        small.append(go(ids_in, ig.at[j], peer))

    def arrive(copies):
        for copy in copies:
            copy.wait_recv()

    def first_ring(step, me, device, own, slot):
        out = [go(own if step == 1 else slot(2 * step - 3), slot(2 * step - 1), device((me + fwd + 8) % 8))]
        if step <= 3:
            out.append(go(own if step == 1 else slot(2 * step - 2), slot(2 * step), device((me - fwd + 8) % 8)))
        return out

    pieces = ((0, 3), (3, 2), (5, 3))

    def second_ring(step, piece, me, device, buf):
        start, size = pieces[piece]
        b = (me - fwd * (step - 1) + 16) % 8
        block = buf.at[b, pl.ds(start, size)]
        out = [go(block, block, device((me + fwd + 8) % 8))]
        if step <= 3:
            b = (me + fwd * (step - 1) + 16) % 8
            block = buf.at[b, pl.ds(start, size)]
            out.append(go(block, block, device((me - fwd + 8) % 8)))
        return out

    def place_of(t, me):
        away = ((t - me) * fwd + 8) % 8
        return 2 * away - (away // 4) * (4 * away - 15)

    a1 = lambda s: first_ring(s, z, dev_z, wa_in, lambda p: wa.at[y, p])
    b1 = lambda s: first_ring(s, y, dev_y, wb_in, lambda p: wb.at[z, p])
    a2 = lambda s, p: second_ring(s, p, y, dev_y, wa)
    b2 = lambda s, p: second_ring(s, p, z, dev_z, wb)

    right, left = (2 * ((x + 1) % NX) + c), (2 * ((x + 3) % NX) + c)
    opposite, sibling = (2 * ((x + 2) % NX) + c), (2 * x + 1 - c)

    def along_x_start(whole_in, half_in, half, whole):
        r0 = go(half_in(0), half(j, 0), dev_e(right))
        l1 = go(half_in(1), half(j, 1), dev_e(left))
        r1 = go(half_in(1), half(j, 1), dev_e(right))
        l0 = go(half_in(0), half(j, 0), dev_e(left))
        s = go(whole_in, whole(j), dev_e(sibling))
        return r0, l1, r1, l0, s

    def along_x_forward(first, half, whole):
        r0, l1, r1, l0, s = first
        r0.wait_recv()
        f0 = go(half(left, 0), half(left, 0), dev_e(right))
        l1.wait_recv()
        f1 = go(half(right, 1), half(right, 1), dev_e(left))
        return f0, f1, r1, l0, s

    def along_x_across(second, whole):
        f0, f1, r1, l0, s = second
        r1.wait_recv()
        s0 = go(whole(left), whole(left), dev_e(sibling))
        l0.wait_recv()
        s1 = go(whole(right), whole(right), dev_e(sibling))
        return f0, f1, s0, s1, s

    def along_x_last(second, half, whole):
        f0, f1, s0, s1, s = second
        f0.wait_recv()
        f1.wait_recv()
        s2 = go(whole(opposite), whole(opposite), dev_e(sibling))
        return s, s0, s1, s2

    f_half = lambda b, h: fg.at[b, pl.ds(64 * h, 64)]
    f_whole = lambda b: fg.at[b]
    w3 = lambda buf: (
        (lambda b, h: buf.at[pl.ds(3 * b, 3), pl.ds(32 * h, 32)]),
        (lambda b: buf.at[pl.ds(3 * b, 3)]),
    )
    e_half, e_whole = w3(eg)
    d_half, d_whole = w3(dg)

    ra, rb = a1(1), b1(1)
    fx = along_x_start(f_in, lambda h: f_in.at[pl.ds(64 * h, 64)], f_half, f_whole)
    ex = along_x_start(enc_in, lambda h: enc_in.at[:, pl.ds(32 * h, 32)], e_half, e_whole)

    wa[y, 0] = wa_in[...]
    wb[z, 0] = wb_in[...]
    fg[j] = f_in[...]
    eg[pl.ds(3 * j, 3)] = enc_in[...]
    dg[pl.ds(3 * j, 3)] = dec_in[...]
    nzg[j] = nz_in[...]
    cg[j] = code_in[...]
    ig[j] = ids_in[...]

    ring = []
    for step in (1, 2, 3, 4):
        arrive(ra)
        arrive(rb)
        if step < 4:
            ra, rb = a1(step + 1), b1(step + 1)
        if step != 3:
            piece = len(ring)
            ring.append((a2(1, piece), b2(1, piece)))
    fx = along_x_forward(fx, f_half, f_whole)

    def kv_part(b):
        rows = jnp.concatenate([wa[b, place_of(t, z)] for t in range(8)], axis=0)
        return mm(fg[b], rows)

    def encode(p, carry):
        enc = mm(two_spans(nzg[p]), weights_of(eg, p)).astype(BF).astype(F32)
        code = cg[p]
        for q in range(2):
            row = jnp.concatenate([code[4 * q + r : 4 * q + r + 1] for r in range(4)], axis=1)
            hid[pl.ds(pl.multiple_of(p * 128 + 64 * q, 64), 64), :] = (enc[64 * q : 64 * q + 64] + row).astype(BF)
        return carry

    def two_spans(pair):
        zero = jnp.zeros_like(pair)
        return jnp.concatenate([jnp.where(lane < STEPS, pair, zero), jnp.where(lane >= STEPS, pair, zero)], axis=0)

    def weights_of(buf, p):
        return jnp.concatenate([buf[ids[p, 0, 0]], buf[ids[p, 0, 1]]], axis=0)

    for step in (2, 3, 4):
        later = []
        for piece in range(3):
            for copies in ring[piece]:
                arrive(copies)
            later.append((a2(step, piece), b2(step, piece)))
        ring = later
        if step == 2:
            fx = along_x_across(fx, f_whole)
            ex = along_x_forward(ex, e_half, e_whole)
            dx = along_x_start(dec_in, lambda h: dec_in.at[:, pl.ds(32 * h, 32)], d_half, d_whole)
        if step == 3:
            fx = along_x_last(fx, f_half, f_whole)
            ex = along_x_across(ex, e_whole)
    arrive(small)
    table = pltpu.make_async_copy(ig, ids, local_sem)
    table.start()
    table.wait()
    arrive(fx)
    kv[:, 0:256] = kv_part(y)
    for step in (1, 2, 3):
        kv[:, 0:256] += kv_part((y - fwd * step + 16) % 8) + kv_part((y + fwd * step + 16) % 8)
    ex = along_x_last(ex, e_half, e_whole)
    arrive(ex)
    lax.fori_loop(0, ne, encode, 0)
    dx = along_x_forward(dx, d_half, d_whole)
    for piece in range(3):
        for copies in ring[piece]:
            arrive(copies)
    dx = along_x_across(dx, d_whole)
    kv[:, 0:256] += kv_part((y + 4) % 8)

    def kv_rest(b, total):
        return total + mm(fg[b], wb[:, place_of(b, y), 0:RK, :].reshape(8 * RK, 128))

    kv[:, 256:384] = lax.fori_loop(0, 8, kv_rest, jnp.zeros((GROUP * CTX, 128), F32))

    def unpack(zz, carry):
        for yy in range(NY):
            tiles = wb[zz, place_of(yy, y), RK:RB, :].astype(F32)
            qo[yy * NZ + zz] = jnp.concatenate([tiles[24 * r : 24 * r + 24] for r in range(3)], axis=1)
        return carry

    lax.fori_loop(0, NZ, unpack, 0)

    def split(b, carry):
        rows = qo[pl.ds(8 * b, 8)].reshape(HC, 2 * HC)
        wq[pl.ds(pl.multiple_of(HC * b, HC), HC), :] = rows[:, :HC].astype(BF)
        wo[pl.ds(pl.multiple_of(HC * b, HC), HC), :] = jnp.concatenate([rows[:, 256:], rows[:, HC:256]], axis=1).astype(BF)
        return carry

    lax.fori_loop(0, NY, split, 0)

    head_of_row = lax.broadcasted_iota(jnp.int32, (32, HC), 0) >> 3
    column = lax.broadcasted_iota(jnp.int32, (32, HC), 1)
    low = head_of_row * HD
    head_mask = jnp.where((column >= low) & (column < low + HD), 1.0, 0.0).astype(F32)

    def spread(flat):
        three = flat.astype(BF).astype(F32).reshape(GROUP, CTX, HC)
        return (jnp.concatenate([three] * 4, axis=1) * head_mask[None]).astype(BF)

    kb[...] = spread(kv[:, :HC])
    vb[...] = spread(kv[:, HC:])

    same_head = jnp.where(
        (lax.broadcasted_iota(jnp.int32, (32, 32), 0) >> 3)
        == (lax.broadcasted_iota(jnp.int32, (32, 32), 1) >> 3), 1.0, 0.0,
    ).astype(F32)

    def head_sum(values):
        return jnp.dot(values, same_head, precision=lax.Precision.HIGHEST, preferred_element_type=F32)

    scale = 1.0 / math.sqrt(HD)

    def attend(g, carry):
        here = pl.ds(pl.multiple_of(256 * g, 256), 256)
        queries = mm(hid[here, :], wq[...]).astype(BF)
        scores = jnp.concatenate([mm_nt(queries[64 * s : 64 * s + 64], kb[4 * g + s]) for s in range(4)], axis=0) * scale
        raised = jnp.exp(scores)
        probs = raised / head_sum(raised)
        prs[here, :] = probs
        rounded = probs.astype(BF)
        out = jnp.concatenate([mm(rounded[64 * s : 64 * s + 64], vb[4 * g + s]) for s in range(4)], axis=0)
        att[here, :] = out.astype(BF)
        att_t[:, here] = out.T.astype(BF)
        return carry

    lax.fori_loop(0, 3, attend, 0)
    dx = along_x_last(dx, d_half, d_whole)
    lax.fori_loop(3, 4, attend, 0)
    arrive(dx)

    def four_decoders(g):
        return jnp.concatenate([weights_of(dg, 2 * g), weights_of(dg, 2 * g + 1)], axis=0)

    shares = []
    for k in (1, 2, 3, 0):
        g = (x + k) % NX
        here = pl.ds(pl.multiple_of(256 * g, 256), 256)
        branch = mm_nt(att[here, :], wo[...])
        if k == 0:
            row_pair = lax.broadcasted_iota(jnp.int32, (256, H), 0) >> 7
            branch += jnp.where(row_pair == c, hid[here, :].astype(F32), 0.0)
        product = mm_nt(branch.astype(BF), four_decoders(g))
        for r in range(2):
            block = product[128 * r : 128 * r + 128, 128 * r : 128 * r + 128]
            ps[2 * g + r] = jnp.where(lane < STEPS, block[0:STEPS], block[STEPS : 2 * STEPS]).astype(BF)
        for r in range(2):
            if k or r:
                p = 2 * g + (c + r) % 2
                shares.append(go(ps.at[p], pr.at[len(shares)], dev_e(p)))
    arrive(shares)
    predicted = ps[j].astype(F32)
    for k in range(1, ne):
        predicted += pr[k - 1].astype(F32)
    low_lane = lane[0:1] < STEPS
    length = jnp.where(low_lane, lengths[0].astype(F32), lengths[1].astype(F32))
    dims = jnp.where(low_lane, act_dims[emb_ids[0]].astype(F32), act_dims[emb_ids[1]].astype(F32))
    step_row = lax.broadcasted_iota(jnp.int32, (STEPS, 2 * STEPS), 0).astype(F32)
    step_col = (lane & (STEPS - 1)).astype(F32)
    valid = jnp.where((step_row < length) & (step_col < dims), 1.0, 0.0).astype(F32)
    error = predicted - vel_in[...]
    squares = jnp.sum(valid * error * error, axis=0, keepdims=True)
    sums = [jnp.sum(jnp.where(half_lanes, squares, 0.0), axis=1, keepdims=True) for half_lanes in (low_lane, ~low_lane)]
    one = [sums[q] / jnp.full((1, 1), lengths[q].astype(F32), F32) for q in range(2)]
    loss_out[...] = jnp.where(id_lane == 0, one[0], one[1])
    dp_own[...] = (2.0 * valid * error / length).astype(BF)
    errors = [go(dp_own, dpg.at[j], dev_e((j + k) % ne)) for k in range(1, ne)]
    dpg[j] = dp_own[...]
    arrive(errors)

    def d_branch(g, carry):
        upper, lower = two_spans(dpg[2 * g]), two_spans(dpg[2 * g + 1])
        zero = jnp.zeros_like(upper)
        left_rows = jnp.concatenate(
            [jnp.concatenate([upper, zero], axis=1), jnp.concatenate([zero, lower], axis=1)], axis=0
        )
        dbr[pl.ds(pl.multiple_of(256 * g, 256), 256), :] = mm(left_rows, four_decoders(g)).astype(BF)
        return carry

    lax.fori_loop(0, 4, d_branch, 0)

    first_of = ((y, dev_y), (z, dev_z))

    def scatter(n, left_t, right_rows):
        for q in range(4):
            part = mm(left_t[...], right_rows[:, 384 * q : 384 * q + 384])
            wide[q] = part
            gs[n, q] = part.astype(BF)
        out = []
        for k in (4, 3, 5, 2, 6, 1, 7):
            for h, (me, device) in enumerate(first_of):
                t = (me + k) % 8
                rows = pl.ds(pl.multiple_of(96 * h + 48 * (t // 4), 16), 48)
                out.append(go(gs.at[n, t % 4, rows], gr.at[n, h, k - 1], device(t)))
        for h, (me, device) in enumerate(first_of):
            own_slice[n, h] = wide[me % 4, pl.ds(pl.multiple_of(96 * h + 48 * (me // 4), 16), 48), :]
        return out

    go_copies = scatter(1, att_t, dbr)

    def back(g, carry):
        here = pl.ds(pl.multiple_of(256 * g, 256), 256)
        d_att = mm(dbr[here, :], wo[...]).astype(BF)
        d_probs = jnp.concatenate([mm_nt(d_att[64 * s : 64 * s + 64], vb[4 * g + s]) for s in range(4)], axis=0)
        probs = prs[here, :]
        d_scores = (probs * (d_probs - head_sum(probs * d_probs))).astype(BF)
        out = jnp.concatenate([mm(d_scores[64 * s : 64 * s + 64], kb[4 * g + s]) for s in range(4)], axis=0) * scale
        dq_t[:, here] = out.T.astype(BF)
        return carry

    lax.fori_loop(0, 4, back, 0)
    gq_copies = scatter(0, dq_t, hid)

    def add_up(n, copies):
        arrive(copies)
        out = []
        for h in range(2):
            total = own_slice[n, h]
            for k in range(7):
                total += gr[n, h, k].astype(F32)
            for t in range(9):
                sb[n, h, t] = total[16 * (t // 3) : 16 * (t // 3) + 16, 128 * (t % 3) : 128 * (t % 3) + 128].astype(BF)
            me, device = first_of[1 - h]
            for k in range(1, 8):
                t = (me + k) % 8
                out.append(go(sb.at[n, h, pl.ds(2 * t, 2)], sr.at[n, h, k - 1], device(t)))
        return out

    def finish(n, copies):
        arrive(copies)
        out = []
        for h in range(2):
            me, device = first_of[1 - h]
            total = sb[n, h, pl.ds(2 * me, 2)].astype(F32)
            for k in range(7):
                total += sr[n, h, k].astype(F32)
            fs[n, h] = total.astype(BF)
            out += [go(fs.at[n, h], sg.at[n, h, pl.ds(2 * me, 2)], device((me + k) % 8)) for k in range(1, 8)]
            sg[n, h, pl.ds(2 * me, 2)] = fs[n, h]
        return out

    def gather(n, step, copies):
        arrive(copies)
        out = []
        for h, (me, device) in enumerate(first_of):
            b = (me - fwd * (step - 1) + 16) % 8
            first = sg.at[n, h, pl.ds(0, 9)]
            out.append(go(first if step == 1 else og.at[n, h, b], og.at[n, h, b], device((me + fwd + 8) % 8)))
            if step <= 3:
                b = (me + fwd * (step - 1) + 16) % 8
                out.append(go(first if step == 1 else og.at[n, h, b], og.at[n, h, b], device((me - fwd + 8) % 8)))
            if step == 1:
                og[n, h, me] = sg[n, h, 0:9]
        return out

    def write(n, out):
        for h in range(2):
            for t in range(8):
                for r in range(9):
                    row, column = 96 * h + 48 * (t // 4) + 16 * (r // 3), 384 * (t % 4) + 128 * (r % 3)
                    out[row : row + 16, column : column + 128] = og[n, h, t, r]

    sb[:, :, 9:16] = jnp.zeros((2, 2, 7, 16, 128), BF)
    go_copies = add_up(1, go_copies)
    go_copies = finish(1, go_copies)
    gq_copies = add_up(0, gq_copies)
    go_copies = gather(1, 1, go_copies)
    gq_copies = finish(0, gq_copies)
    go_copies = gather(1, 2, go_copies)
    gq_copies = gather(0, 1, gq_copies)
    go_copies = gather(1, 3, go_copies)
    gq_copies = gather(0, 2, gq_copies)
    go_copies = gather(1, 4, go_copies)
    gq_copies = gather(0, 3, gq_copies)
    arrive(go_copies)
    gq_copies = gather(0, 4, gq_copies)
    write(1, go_out)
    arrive(gq_copies)
    write(0, gq_out)
    for copy in cs.made:
        copy.wait_send()


def widen(q_in, o_in, loss_in, q_out, o_out, loss_out):
    q_out[...] = q_in[...].astype(F32)
    o_out[...] = o_in[...].astype(F32)
    for q in range(2):
        loss_out[q] = loss_in[0, q]


def body(actions, noise, emb_ids, lengths, t_index, act_dims, features, enc_w, dec_w, wq, wk, wv, wo_t):
    vm = pl.BlockSpec(memory_space=pltpu.VMEM)
    sm = pl.BlockSpec(memory_space=pltpu.SMEM)
    V = pltpu.VMEM
    d_q, d_o, loss = pl.pallas_call(
        kernel,
        out_shape=(
            jax.ShapeDtypeStruct((HC, H), BF),
            jax.ShapeDtypeStruct((HC, H), BF),
            jax.ShapeDtypeStruct((8, 128), F32),
        ),
        in_specs=[vm] * 2 + [sm] * 4 + [vm] * 7,
        out_specs=(vm, vm, vm),
        scratch_shapes=[
            V((RK, 256), BF),
            V((RB, 128), BF),
            V((STEPS, 128), BF),
            V((STEPS, 128), F32),
            V((8, 384), F32),
            V((8, 128), jnp.int32),
            V((NY, NZ, RK, 256), BF),
            V((NZ, NY, RB, 128), BF),
            V((8, GROUP * CTX, 640), BF),
            V((EMBS, STEPS, H), BF),
            V((EMBS, STEPS, H), BF),
            V((8, STEPS, 128), BF),
            V((8, 8, 384), F32),
            V((8, 8, 128), jnp.int32),
            pltpu.SMEM((8, 8, 128), jnp.int32),
            V((GROUP * CTX, 2 * HC), F32),
            V((64, 24, 2 * HC), F32),
            V((H, HC), BF),
            V((H, HC), BF),
            V((GROUP, 32, HC), BF),
            V((GROUP, 32, HC), BF),
            V((ROWS, H), BF),
            V((ROWS, H), BF),
            V((ROWS, 32), F32),
            V((ROWS, HC), BF),
            V((HC, ROWS), BF),
            V((HC, ROWS), BF),
            V((8, STEPS, 128), BF),
            V((7, STEPS, 128), BF),
            V((STEPS, 128), BF),
            V((8, STEPS, 128), BF),
            V((2, 4, HC, 384), BF),
            V((4, HC, 384), F32),
            V((2, 2, 48, 384), F32),
            V((2, 2, 7, 48, 384), BF),
            V((2, 2, 16, 16, 128), BF),
            V((2, 2, 7, 2, 16, 128), BF),
            V((2, 2, 2, 16, 128), BF),
            V((2, 2, 16, 16, 128), BF),
            V((2, 2, 8, 9, 16, 128), BF),
            pltpu.SemaphoreType.DMA((N_COPIES,)),
            pltpu.SemaphoreType.DMA((N_COPIES,)),
            pltpu.SemaphoreType.DMA,
        ],
        compiler_params=pltpu.CompilerParams(
            collective_id=0, has_side_effects=True, vmem_limit_bytes=56 * 1024 * 1024
        ),
    )(
        actions, noise, emb_ids, lengths, t_index, act_dims, features.reshape(GROUP * CTX, 640), enc_w,
        jnp.swapaxes(dec_w, 1, 2), wq, wk, wv, wo_t,
    )
    return pl.pallas_call(
        widen,
        out_shape=(
            jax.ShapeDtypeStruct((HC, H), F32), jax.ShapeDtypeStruct((HC, H), F32), jax.ShapeDtypeStruct((2,), F32),
        ),
        in_specs=[vm, vm, sm],
        out_specs=(vm, vm, sm),
    )(d_q, d_o, loss)


def solution(mesh):
    rows = P(("dp", "emb"))
    in_specs = (
        P(("dp", "emb"), None, None), P(("dp", "emb"), None, None), rows, rows, rows, P(),
        P("dp", None, "emb"), P("emb", None, None), P("emb", None, None),
        P("dp", "emb"), P("dp", "emb"), P("dp", "emb"), P("dp", "emb"),
    )
    out_specs = (P("emb", None), P("emb", None), rows)
    return jax.shard_map(body, mesh=mesh, in_specs=in_specs, out_specs=out_specs, check_vma=False)
```

```python
import functools
import math

import jax
import jax.numpy as jnp
from jax import lax
from jax.experimental import pallas as pl
from jax.experimental.pallas import tpu as pltpu
from jax.sharding import PartitionSpec as P

HD = 48
TSTEPS = 1000
H = 1536
HC = 192
STEPS = 64
EMBS = 24
NY = 8
NZ = 8
NX = 4
GROUP = 16
CTX = 8
ROWS = GROUP * STEPS
RK = 80
RB = 160
MESH = pl.DeviceIdType.MESH
BF = jnp.bfloat16
F32 = jnp.float32
NT = (((1,), (1,)), ((), ()))


def mm(a, b):
    return jnp.dot(a, b, preferred_element_type=F32)


def mm_nt(a, b):
    return lax.dot_general(a, b, NT, preferred_element_type=F32)


class Copies:
    def __init__(self, send, recv):
        self.send, self.recv, self.count, self.made = send, recv, 0, []

    def make(self, src, dst, device):
        k = self.count
        self.count += 1
        copy = pltpu.make_async_remote_copy(
            src_ref=src, dst_ref=dst, send_sem=self.send.at[k], recv_sem=self.recv.at[k],
            device_id=device, device_id_type=MESH,
        )
        copy.start()
        self.made.append(copy)
        return copy


N_COPIES = 256


def kernel(
    act, noise, emb_ids, lengths, levels, act_dims, f_in, enc_in, dec_in, wq_own, wk_own, wv_own, wo_own,
    gq_out, go_out, loss_out,
    wa_in, wb_in, nz_in, vel_in, code_in, ids_in,
    wa, wb, fg, eg, dg, nzg, cg, ig, ids, kv, qo, wq, wo, kb, vb,
    hid, dbr, prs, att, att_t, dq_t, ps, pr, dp_own, dpg,
    gs, wide, own_slice, gr, sb, sr, fs, sg, og, send_sems, recv_sems, local_sem,
):
    i = lax.axis_index("dp")
    j = lax.axis_index("emb")
    y, z = i // NZ, i % NZ
    x, c = j // 2, j % 2
    ne = 2 * NX

    barrier = pltpu.get_barrier_semaphore()
    for k in range(1, ne):
        pl.semaphore_signal(barrier, inc=1, device_id=(i, (j + k) % ne), device_id_type=MESH)
    for k in range(1, NY):
        pl.semaphore_signal(barrier, inc=1, device_id=(((y + k) % NY) * NZ + z, j), device_id_type=MESH)
    for k in range(1, NZ):
        pl.semaphore_signal(barrier, inc=1, device_id=(y * NZ + (z + k) % NZ, j), device_id_type=MESH)

    wa_in[...] = jnp.concatenate([wk_own[...], wv_own[:, :STEPS]], axis=1)
    wb_in[0:RK, :] = wv_own[:, STEPS:]
    q_own, o_own = wq_own[...].astype(F32), wo_own[...].astype(F32)
    wb_in[RK:RB, :] = jnp.concatenate(
        [q_own[:, :128], jnp.concatenate([q_own[:, 128:], o_own[:, 128:]], axis=1), o_own[:, :128],
         jnp.zeros((8, 128), F32)], axis=0,
    ).astype(BF)
    lane = lax.broadcasted_iota(jnp.int32, (STEPS, 2 * STEPS), 1)
    mixed = []
    for q in range(2):
        fraction = jnp.full((STEPS, STEPS), levels[q].astype(F32), F32) / TSTEPS
        mixed.append((1.0 - fraction) * noise[q].astype(F32) + fraction * act[q].astype(F32))
    nz_in[...] = jnp.concatenate(mixed, axis=1).astype(BF)
    vel_in[...] = jnp.concatenate([act[q].astype(F32) - noise[q].astype(F32) for q in range(2)], axis=1)
    code_row = lax.broadcasted_iota(jnp.int32, (8, 384), 0)
    code_lane = lax.broadcasted_iota(jnp.int32, (8, 384), 1)
    half = H // 2
    freq = jnp.exp(-math.log(10000.0) * (code_lane + 384 * (code_row & 1)).astype(F32) / half)
    level = jnp.where(code_row < 4, levels[0].astype(F32), levels[1].astype(F32))
    angle = level * freq
    code_in[...] = jnp.where((code_row & 2) == 0, jnp.sin(angle), jnp.cos(angle))
    id_lane = lax.broadcasted_iota(jnp.int32, (8, 128), 1)
    ids_in[...] = jnp.where(id_lane == 0, emb_ids[0], emb_ids[1])

    pl.semaphore_wait(barrier, (ne - 1) + (NY - 1) + (NZ - 1))

    cs = Copies(send_sems, recv_sems)
    go = cs.make
    dev_y = lambda t: (t * NZ + z, j)
    dev_z = lambda t: (y * NZ + t, j)
    dev_e = lambda t: (i, t)
    fwd = 1 - 2 * c

    small = []
    for k in range(1, ne):
        peer = dev_e((j + k) % ne)
        small.append(go(nz_in, nzg.at[j], peer))
        small.append(go(code_in, cg.at[j], peer))
        small.append(go(ids_in, ig.at[j], peer))

    def arrive(copies):
        for copy in copies:
            copy.wait_recv()

    def first_ring(step, me, device, own, slot):
        out = [go(own if step == 1 else slot(2 * step - 3), slot(2 * step - 1), device((me + fwd + 8) % 8))]
        if step <= 3:
            out.append(go(own if step == 1 else slot(2 * step - 2), slot(2 * step), device((me - fwd + 8) % 8)))
        return out

    pieces = ((0, 3), (3, 2), (5, 3))

    def second_ring(step, piece, me, device, buf):
        start, size = pieces[piece]
        b = (me - fwd * (step - 1) + 16) % 8
        block = buf.at[b, pl.ds(start, size)]
        out = [go(block, block, device((me + fwd + 8) % 8))]
        if step <= 3:
            b = (me + fwd * (step - 1) + 16) % 8
            block = buf.at[b, pl.ds(start, size)]
            out.append(go(block, block, device((me - fwd + 8) % 8)))
        return out

    def place_of(t, me):
        away = ((t - me) * fwd + 8) % 8
        return 2 * away - (away // 4) * (4 * away - 15)

    a1 = lambda s: first_ring(s, z, dev_z, wa_in, lambda p: wa.at[y, p])
    b1 = lambda s: first_ring(s, y, dev_y, wb_in, lambda p: wb.at[z, p])
    a2 = lambda s, p: second_ring(s, p, y, dev_y, wa)
    b2 = lambda s, p: second_ring(s, p, z, dev_z, wb)

    right, left = (2 * ((x + 1) % NX) + c), (2 * ((x + 3) % NX) + c)
    opposite, sibling = (2 * ((x + 2) % NX) + c), (2 * x + 1 - c)

    def along_x_start(whole_in, half_in, half, whole):
        r0 = go(half_in(0), half(j, 0), dev_e(right))
        l1 = go(half_in(1), half(j, 1), dev_e(left))
        r1 = go(half_in(1), half(j, 1), dev_e(right))
        l0 = go(half_in(0), half(j, 0), dev_e(left))
        s = go(whole_in, whole(j), dev_e(sibling))
        return r0, l1, r1, l0, s

    def along_x_forward(first, half, whole):
        r0, l1, r1, l0, s = first
        r0.wait_recv()
        f0 = go(half(left, 0), half(left, 0), dev_e(right))
        l1.wait_recv()
        f1 = go(half(right, 1), half(right, 1), dev_e(left))
        return f0, f1, r1, l0, s

    def along_x_across(second, whole):
        f0, f1, r1, l0, s = second
        r1.wait_recv()
        s0 = go(whole(left), whole(left), dev_e(sibling))
        l0.wait_recv()
        s1 = go(whole(right), whole(right), dev_e(sibling))
        return f0, f1, s0, s1, s

    def along_x_last(second, half, whole):
        f0, f1, s0, s1, s = second
        f0.wait_recv()
        f1.wait_recv()
        s2 = go(whole(opposite), whole(opposite), dev_e(sibling))
        return s, s0, s1, s2

    f_half = lambda b, h: fg.at[b, pl.ds(64 * h, 64)]
    f_whole = lambda b: fg.at[b]
    w3 = lambda buf: (
        (lambda b, h: buf.at[pl.ds(3 * b, 3), pl.ds(32 * h, 32)]),
        (lambda b: buf.at[pl.ds(3 * b, 3)]),
    )
    e_half, e_whole = w3(eg)
    d_half, d_whole = w3(dg)

    ra, rb = a1(1), b1(1)
    fx = along_x_start(f_in, lambda h: f_in.at[pl.ds(64 * h, 64)], f_half, f_whole)
    ex = along_x_start(enc_in, lambda h: enc_in.at[:, pl.ds(32 * h, 32)], e_half, e_whole)

    wa[y, 0] = wa_in[...]
    wb[z, 0] = wb_in[...]
    fg[j] = f_in[...]
    eg[pl.ds(3 * j, 3)] = enc_in[...]
    dg[pl.ds(3 * j, 3)] = dec_in[...]
    nzg[j] = nz_in[...]
    cg[j] = code_in[...]
    ig[j] = ids_in[...]

    ring = []
    for step in (1, 2, 3, 4):
        arrive(ra)
        arrive(rb)
        if step < 4:
            ra, rb = a1(step + 1), b1(step + 1)
        if step != 3:
            piece = len(ring)
            ring.append((a2(1, piece), b2(1, piece)))
    fx = along_x_forward(fx, f_half, f_whole)

    def kv_part(b):
        rows = jnp.concatenate([wa[b, place_of(t, z)] for t in range(8)], axis=0)
        return mm(fg[b], rows)

    def encode(p, carry):
        enc = mm(two_spans(nzg[p]), weights_of(eg, p)).astype(BF).astype(F32)
        code = cg[p]
        for q in range(2):
            row = jnp.concatenate([code[4 * q + r : 4 * q + r + 1] for r in range(4)], axis=1)
            hid[pl.ds(pl.multiple_of(p * 128 + 64 * q, 64), 64), :] = (enc[64 * q : 64 * q + 64] + row).astype(BF)
        return carry

    def two_spans(pair):
        zero = jnp.zeros_like(pair)
        return jnp.concatenate([jnp.where(lane < STEPS, pair, zero), jnp.where(lane >= STEPS, pair, zero)], axis=0)

    def weights_of(buf, p):
        return jnp.concatenate([buf[ids[p, 0, 0]], buf[ids[p, 0, 1]]], axis=0)

    for step in (2, 3, 4):
        later = []
        for piece in range(3):
            for copies in ring[piece]:
                arrive(copies)
            later.append((a2(step, piece), b2(step, piece)))
        ring = later
        if step == 2:
            fx = along_x_across(fx, f_whole)
            ex = along_x_forward(ex, e_half, e_whole)
            dx = along_x_start(dec_in, lambda h: dec_in.at[:, pl.ds(32 * h, 32)], d_half, d_whole)
        if step == 3:
            fx = along_x_last(fx, f_half, f_whole)
            ex = along_x_across(ex, e_whole)
    arrive(small)
    table = pltpu.make_async_copy(ig, ids, local_sem)
    table.start()
    table.wait()
    arrive(fx)
    kv[:, 0:256] = kv_part(y)
    for step in (1, 2, 3):
        kv[:, 0:256] += kv_part((y - fwd * step + 16) % 8) + kv_part((y + fwd * step + 16) % 8)
    ex = along_x_last(ex, e_half, e_whole)
    arrive(ex)
    lax.fori_loop(0, ne, encode, 0)
    dx = along_x_forward(dx, d_half, d_whole)
    for piece in range(3):
        for copies in ring[piece]:
            arrive(copies)
    dx = along_x_across(dx, d_whole)
    kv[:, 0:256] += kv_part((y + 4) % 8)

    def kv_rest(b, total):
        return total + mm(fg[b], wb[:, place_of(b, y), 0:RK, :].reshape(8 * RK, 128))

    kv[:, 256:384] = lax.fori_loop(0, 8, kv_rest, jnp.zeros((GROUP * CTX, 128), F32))

    def unpack(zz, carry):
        for yy in range(NY):
            tiles = wb[zz, place_of(yy, y), RK:RB, :].astype(F32)
            qo[yy * NZ + zz] = jnp.concatenate([tiles[24 * r : 24 * r + 24] for r in range(3)], axis=1)
        return carry

    lax.fori_loop(0, NZ, unpack, 0)

    def split(b, carry):
        rows = qo[pl.ds(8 * b, 8)].reshape(HC, 2 * HC)
        wq[pl.ds(pl.multiple_of(HC * b, HC), HC), :] = rows[:, :HC].astype(BF)
        wo[pl.ds(pl.multiple_of(HC * b, HC), HC), :] = jnp.concatenate([rows[:, 256:], rows[:, HC:256]], axis=1).astype(BF)
        return carry

    lax.fori_loop(0, NY, split, 0)

    head_of_row = lax.broadcasted_iota(jnp.int32, (32, HC), 0) >> 3
    column = lax.broadcasted_iota(jnp.int32, (32, HC), 1)
    low = head_of_row * HD
    head_mask = jnp.where((column >= low) & (column < low + HD), 1.0, 0.0).astype(F32)

    def spread(flat):
        three = flat.astype(BF).astype(F32).reshape(GROUP, CTX, HC)
        return (jnp.concatenate([three] * 4, axis=1) * head_mask[None]).astype(BF)

    kb[...] = spread(kv[:, :HC])
    vb[...] = spread(kv[:, HC:])

    same_head = jnp.where(
        (lax.broadcasted_iota(jnp.int32, (128, 128), 0) >> 3)
        == (lax.broadcasted_iota(jnp.int32, (128, 128), 1) >> 3), 1.0, 0.0,
    ).astype(F32)
    same_span = (lax.broadcasted_iota(jnp.int32, (256, 128), 0) >> 6) == (
        lax.broadcasted_iota(jnp.int32, (256, 128), 1) >> 5
    )

    def four(buf, g):
        return buf[pl.ds(4 * g, 4)].reshape(128, HC)

    def head_sum(values):
        return jnp.dot(values, same_head, precision=lax.Precision.HIGHEST, preferred_element_type=F32)

    scale = 1.0 / math.sqrt(HD)

    def attend(g, carry):
        here = pl.ds(pl.multiple_of(256 * g, 256), 256)
        queries = mm(hid[here, :], wq[...]).astype(BF)
        scores = jnp.where(same_span, mm_nt(queries, four(kb, g)) * scale, 0.0)
        raised = jnp.exp(scores)
        probs = jnp.where(same_span, raised / head_sum(raised), 0.0)
        prs[here, :] = probs
        out = mm(probs.astype(BF), four(vb, g))
        att[here, :] = out.astype(BF)
        att_t[:, here] = out.T.astype(BF)
        return carry

    lax.fori_loop(0, 3, attend, 0)
    dx = along_x_last(dx, d_half, d_whole)
    lax.fori_loop(3, 4, attend, 0)
    arrive(dx)

    def four_decoders(g):
        return jnp.concatenate([weights_of(dg, 2 * g), weights_of(dg, 2 * g + 1)], axis=0)

    shares = []
    for k in (1, 2, 3, 0):
        g = (x + k) % NX
        here = pl.ds(pl.multiple_of(256 * g, 256), 256)
        branch = mm_nt(att[here, :], wo[...])
        if k == 0:
            row_pair = lax.broadcasted_iota(jnp.int32, (256, H), 0) >> 7
            branch += jnp.where(row_pair == c, hid[here, :].astype(F32), 0.0)
        product = mm_nt(branch.astype(BF), four_decoders(g))
        for r in range(2):
            block = product[128 * r : 128 * r + 128, 128 * r : 128 * r + 128]
            ps[2 * g + r] = jnp.where(lane < STEPS, block[0:STEPS], block[STEPS : 2 * STEPS]).astype(BF)
        for r in range(2):
            if k or r:
                p = 2 * g + (c + r) % 2
                shares.append(go(ps.at[p], pr.at[len(shares)], dev_e(p)))
    arrive(shares)
    predicted = ps[j].astype(F32)
    for k in range(1, ne):
        predicted += pr[k - 1].astype(F32)
    low_lane = lane[0:1] < STEPS
    length = jnp.where(low_lane, lengths[0].astype(F32), lengths[1].astype(F32))
    dims = jnp.where(low_lane, act_dims[emb_ids[0]].astype(F32), act_dims[emb_ids[1]].astype(F32))
    step_row = lax.broadcasted_iota(jnp.int32, (STEPS, 2 * STEPS), 0).astype(F32)
    step_col = (lane & (STEPS - 1)).astype(F32)
    valid = jnp.where((step_row < length) & (step_col < dims), 1.0, 0.0).astype(F32)
    error = predicted - vel_in[...]
    squares = jnp.sum(valid * error * error, axis=0, keepdims=True)
    sums = [jnp.sum(jnp.where(half_lanes, squares, 0.0), axis=1, keepdims=True) for half_lanes in (low_lane, ~low_lane)]
    one = [sums[q] / jnp.full((1, 1), lengths[q].astype(F32), F32) for q in range(2)]
    loss_out[...] = jnp.where(id_lane == 0, one[0], one[1])
    dp_own[...] = (2.0 * valid * error / length).astype(BF)
    errors = [go(dp_own, dpg.at[j], dev_e((j + k) % ne)) for k in range(1, ne)]
    dpg[j] = dp_own[...]
    arrive(errors)

    def d_branch(g, carry):
        upper, lower = two_spans(dpg[2 * g]), two_spans(dpg[2 * g + 1])
        zero = jnp.zeros_like(upper)
        left_rows = jnp.concatenate(
            [jnp.concatenate([upper, zero], axis=1), jnp.concatenate([zero, lower], axis=1)], axis=0
        )
        dbr[pl.ds(pl.multiple_of(256 * g, 256), 256), :] = mm(left_rows, four_decoders(g)).astype(BF)
        return carry

    lax.fori_loop(0, 4, d_branch, 0)

    first_of = ((y, dev_y), (z, dev_z))

    def scatter(n, left_t, right_rows):
        for q in range(4):
            part = mm(left_t[...], right_rows[:, 384 * q : 384 * q + 384])
            wide[q] = part
            gs[n, q] = part.astype(BF)
        out = []
        for k in (4, 3, 5, 2, 6, 1, 7):
            for h, (me, device) in enumerate(first_of):
                t = (me + k) % 8
                rows = pl.ds(pl.multiple_of(96 * h + 48 * (t // 4), 16), 48)
                out.append(go(gs.at[n, t % 4, rows], gr.at[n, h, k - 1], device(t)))
        for h, (me, device) in enumerate(first_of):
            own_slice[n, h] = wide[me % 4, pl.ds(pl.multiple_of(96 * h + 48 * (me // 4), 16), 48), :]
        return out

    go_copies = scatter(1, att_t, dbr)

    def back(g, carry):
        here = pl.ds(pl.multiple_of(256 * g, 256), 256)
        d_att = mm(dbr[here, :], wo[...]).astype(BF)
        d_probs = mm_nt(d_att, four(vb, g))
        probs = prs[here, :]
        d_scores = (probs * (d_probs - head_sum(probs * d_probs))).astype(BF)
        out = mm(d_scores, four(kb, g)) * scale
        dq_t[:, here] = out.T.astype(BF)
        return carry

    lax.fori_loop(0, 4, back, 0)
    gq_copies = scatter(0, dq_t, hid)

    def add_up(n, copies):
        arrive(copies)
        out = []
        for h in range(2):
            total = own_slice[n, h]
            for k in range(7):
                total += gr[n, h, k].astype(F32)
            for t in range(9):
                sb[n, h, t] = total[16 * (t // 3) : 16 * (t // 3) + 16, 128 * (t % 3) : 128 * (t % 3) + 128].astype(BF)
            me, device = first_of[1 - h]
            for k in range(1, 8):
                t = (me + k) % 8
                out.append(go(sb.at[n, h, pl.ds(2 * t, 2)], sr.at[n, h, k - 1], device(t)))
        return out

    def finish(n, copies):
        arrive(copies)
        out = []
        for h in range(2):
            me, device = first_of[1 - h]
            total = sb[n, h, pl.ds(2 * me, 2)].astype(F32)
            for k in range(7):
                total += sr[n, h, k].astype(F32)
            fs[n, h] = total.astype(BF)
            out += [go(fs.at[n, h], sg.at[n, h, pl.ds(2 * me, 2)], device((me + k) % 8)) for k in range(1, 8)]
            sg[n, h, pl.ds(2 * me, 2)] = fs[n, h]
        return out

    def gather(n, copies):
        arrive(copies)
        out = []
        for h, (me, device) in enumerate(first_of):
            sent = [
                go(sg.at[n, h, pl.ds(0, 9)], og.at[n, h, me], device((me + fwd * k + 8) % 8)) for k in (2, -2, 1, -1)
            ]
            og[n, h, me] = sg[n, h, 0:9]
            out.append(sent)
        return out

    def gather_on(n, before):
        out = []
        for h, (me, device) in enumerate(first_of):
            ahead, behind, *near = before[h]
            ahead.wait_recv()
            block = og.at[n, h, (me - 2 * fwd + 8) % 8]
            out += [go(block, block, device((me + fwd * k + 8) % 8)) for k in (2, 1)]
            behind.wait_recv()
            block = og.at[n, h, (me + 2 * fwd + 8) % 8]
            out.append(go(block, block, device((me - fwd + 8) % 8)))
            out += near
        return out

    def write(n, out):
        for h in range(2):
            for t in range(8):
                for r in range(9):
                    row, column = 96 * h + 48 * (t // 4) + 16 * (r // 3), 384 * (t % 4) + 128 * (r % 3)
                    out[row : row + 16, column : column + 128] = og[n, h, t, r]

    sb[:, :, 9:16] = jnp.zeros((2, 2, 7, 16, 128), BF)
    go_copies = add_up(1, go_copies)
    go_copies = finish(1, go_copies)
    gq_copies = add_up(0, gq_copies)
    go_copies = gather(1, go_copies)
    gq_copies = finish(0, gq_copies)
    go_copies = gather_on(1, go_copies)
    gq_copies = gather(0, gq_copies)
    arrive(go_copies)
    gq_copies = gather_on(0, gq_copies)
    write(1, go_out)
    arrive(gq_copies)
    write(0, gq_out)
    for copy in cs.made:
        copy.wait_send()


def widen(q_in, o_in, loss_in, q_out, o_out, loss_out):
    q_out[...] = q_in[...].astype(F32)
    o_out[...] = o_in[...].astype(F32)
    for q in range(2):
        loss_out[q] = loss_in[0, q]


def body(actions, noise, emb_ids, lengths, t_index, act_dims, features, enc_w, dec_w, wq, wk, wv, wo_t):
    vm = pl.BlockSpec(memory_space=pltpu.VMEM)
    sm = pl.BlockSpec(memory_space=pltpu.SMEM)
    V = pltpu.VMEM
    d_q, d_o, loss = pl.pallas_call(
        kernel,
        out_shape=(
            jax.ShapeDtypeStruct((HC, H), BF),
            jax.ShapeDtypeStruct((HC, H), BF),
            jax.ShapeDtypeStruct((8, 128), F32),
        ),
        in_specs=[vm] * 2 + [sm] * 4 + [vm] * 7,
        out_specs=(vm, vm, vm),
        scratch_shapes=[
            V((RK, 256), BF),
            V((RB, 128), BF),
            V((STEPS, 128), BF),
            V((STEPS, 128), F32),
            V((8, 384), F32),
            V((8, 128), jnp.int32),
            V((NY, NZ, RK, 256), BF),
            V((NZ, NY, RB, 128), BF),
            V((8, GROUP * CTX, 640), BF),
            V((EMBS, STEPS, H), BF),
            V((EMBS, STEPS, H), BF),
            V((8, STEPS, 128), BF),
            V((8, 8, 384), F32),
            V((8, 8, 128), jnp.int32),
            pltpu.SMEM((8, 8, 128), jnp.int32),
            V((GROUP * CTX, 2 * HC), F32),
            V((64, 24, 2 * HC), F32),
            V((H, HC), BF),
            V((H, HC), BF),
            V((GROUP, 32, HC), BF),
            V((GROUP, 32, HC), BF),
            V((ROWS, H), BF),
            V((ROWS, H), BF),
            V((ROWS, 128), F32),
            V((ROWS, HC), BF),
            V((HC, ROWS), BF),
            V((HC, ROWS), BF),
            V((8, STEPS, 128), BF),
            V((7, STEPS, 128), BF),
            V((STEPS, 128), BF),
            V((8, STEPS, 128), BF),
            V((2, 4, HC, 384), BF),
            V((4, HC, 384), F32),
            V((2, 2, 48, 384), F32),
            V((2, 2, 7, 48, 384), BF),
            V((2, 2, 16, 16, 128), BF),
            V((2, 2, 7, 2, 16, 128), BF),
            V((2, 2, 2, 16, 128), BF),
            V((2, 2, 16, 16, 128), BF),
            V((2, 2, 8, 9, 16, 128), BF),
            pltpu.SemaphoreType.DMA((N_COPIES,)),
            pltpu.SemaphoreType.DMA((N_COPIES,)),
            pltpu.SemaphoreType.DMA,
        ],
        compiler_params=pltpu.CompilerParams(
            collective_id=0, has_side_effects=True, vmem_limit_bytes=56 * 1024 * 1024
        ),
    )(
        actions, noise, emb_ids, lengths, t_index, act_dims, features.reshape(GROUP * CTX, 640), enc_w,
        jnp.swapaxes(dec_w, 1, 2), wq, wk, wv, wo_t,
    )
    return pl.pallas_call(
        widen,
        out_shape=(
            jax.ShapeDtypeStruct((HC, H), F32), jax.ShapeDtypeStruct((HC, H), F32), jax.ShapeDtypeStruct((2,), F32),
        ),
        in_specs=[vm, vm, sm],
        out_specs=(vm, vm, sm),
    )(d_q, d_o, loss)


def solution(mesh):
    rows = P(("dp", "emb"))
    in_specs = (
        P(("dp", "emb"), None, None), P(("dp", "emb"), None, None), rows, rows, rows, P(),
        P("dp", None, "emb"), P("emb", None, None), P("emb", None, None),
        P("dp", "emb"), P("dp", "emb"), P("dp", "emb"), P("dp", "emb"),
    )
    out_specs = (P("emb", None), P("emb", None), rows)
    return jax.shard_map(body, mesh=mesh, in_specs=in_specs, out_specs=out_specs, check_vma=False)
```

```python
import functools
import math

import jax
import jax.numpy as jnp
from jax import lax
from jax.experimental import pallas as pl
from jax.experimental.pallas import tpu as pltpu
from jax.sharding import PartitionSpec as P

HD = 48
TSTEPS = 1000
H = 1536
HC = 192
STEPS = 64
EMBS = 24
NY = 8
NZ = 8
NX = 4
GROUP = 16
CTX = 8
ROWS = GROUP * STEPS
RK = 80
RB = 160
MESH = pl.DeviceIdType.MESH
BF = jnp.bfloat16
F32 = jnp.float32
NT = (((1,), (1,)), ((), ()))


def mm(a, b):
    return jnp.dot(a, b, preferred_element_type=F32)


def mm_nt(a, b):
    return lax.dot_general(a, b, NT, preferred_element_type=F32)


class Copies:
    def __init__(self, send, recv):
        self.send, self.recv, self.count, self.made = send, recv, 0, []

    def make(self, src, dst, device):
        k = self.count
        self.count += 1
        copy = pltpu.make_async_remote_copy(
            src_ref=src, dst_ref=dst, send_sem=self.send.at[k], recv_sem=self.recv.at[k],
            device_id=device, device_id_type=MESH,
        )
        copy.start()
        self.made.append(copy)
        return copy


N_COPIES = 256


def kernel(
    act, noise, emb_ids, lengths, levels, act_dims, f_in, enc_in, dec_in, wq_own, wk_own, wv_own, wo_own,
    gq_out, go_out, loss_out,
    wa_in, wb_in, nz_in, vel_in, freqs, ids_in,
    wa, wb, fg, eg, dg, nzg, ig, ids, kv, qo, wq, wo, kb, vb,
    hid, dbr, prs, att, att_t, dq_t, ps, pr, dp_own, dpg,
    gs, wide, own_slice, gr, sb, sr, fs, sg, og, send_sems, recv_sems, local_sem,
):
    i = lax.axis_index("dp")
    j = lax.axis_index("emb")
    y, z = i // NZ, i % NZ
    x, c = j // 2, j % 2
    ne = 2 * NX

    barrier = pltpu.get_barrier_semaphore()
    for k in range(1, ne):
        pl.semaphore_signal(barrier, inc=1, device_id=(i, (j + k) % ne), device_id_type=MESH)
    for k in range(1, NY):
        pl.semaphore_signal(barrier, inc=1, device_id=(((y + k) % NY) * NZ + z, j), device_id_type=MESH)
    for k in range(1, NZ):
        pl.semaphore_signal(barrier, inc=1, device_id=(y * NZ + (z + k) % NZ, j), device_id_type=MESH)

    wa_in[...] = jnp.concatenate([wk_own[...], wv_own[:, :STEPS]], axis=1)
    wb_in[0:RK, :] = wv_own[:, STEPS:]
    q_own, o_own = wq_own[...].astype(F32), wo_own[...].astype(F32)
    wb_in[RK:RB, :] = jnp.concatenate(
        [q_own[:, :128], jnp.concatenate([q_own[:, 128:], o_own[:, 128:]], axis=1), o_own[:, :128],
         jnp.zeros((8, 128), F32)], axis=0,
    ).astype(BF)
    lane = lax.broadcasted_iota(jnp.int32, (STEPS, 2 * STEPS), 1)
    mixed = []
    for q in range(2):
        fraction = jnp.full((STEPS, STEPS), levels[q].astype(F32), F32) / TSTEPS
        mixed.append((1.0 - fraction) * noise[q].astype(F32) + fraction * act[q].astype(F32))
    nz_in[...] = jnp.concatenate(mixed, axis=1).astype(BF)
    vel_in[...] = jnp.concatenate([act[q].astype(F32) - noise[q].astype(F32) for q in range(2)], axis=1)
    code_row = lax.broadcasted_iota(jnp.int32, (8, 384), 0)
    code_lane = lax.broadcasted_iota(jnp.int32, (8, 384), 1)
    half = H // 2
    freq = jnp.exp(-math.log(10000.0) * (code_lane + 384 * (code_row & 1)).astype(F32) / half)
    freqs[...] = freq
    id_lane = lax.broadcasted_iota(jnp.int32, (8, 128), 1)
    ids_in[...] = jnp.where(
        id_lane < 2, jnp.where(id_lane == 0, emb_ids[0], emb_ids[1]), jnp.where(id_lane == 2, levels[0], levels[1])
    )

    pl.semaphore_wait(barrier, (ne - 1) + (NY - 1) + (NZ - 1))

    cs = Copies(send_sems, recv_sems)
    go = cs.make
    dev_y = lambda t: (t * NZ + z, j)
    dev_z = lambda t: (y * NZ + t, j)
    dev_e = lambda t: (i, t)
    fwd = 1 - 2 * c

    small = []
    for k in range(1, ne):
        peer = dev_e((j + k) % ne)
        small.append(go(nz_in, nzg.at[j], peer))
        small.append(go(ids_in, ig.at[j], peer))

    def arrive(copies):
        for copy in copies:
            copy.wait_recv()

    def first_ring(step, me, device, own, slot):
        out = [go(own if step == 1 else slot(2 * step - 3), slot(2 * step - 1), device((me + fwd + 8) % 8))]
        if step <= 3:
            out.append(go(own if step == 1 else slot(2 * step - 2), slot(2 * step), device((me - fwd + 8) % 8)))
        return out

    pieces = ((0, 3), (3, 2), (5, 3))

    def second_ring(step, piece, me, device, buf):
        start, size = pieces[piece]
        b = (me - fwd * (step - 1) + 16) % 8
        block = buf.at[b, pl.ds(start, size)]
        out = [go(block, block, device((me + fwd + 8) % 8))]
        if step <= 3:
            b = (me + fwd * (step - 1) + 16) % 8
            block = buf.at[b, pl.ds(start, size)]
            out.append(go(block, block, device((me - fwd + 8) % 8)))
        return out

    def place_of(t, me):
        away = ((t - me) * fwd + 8) % 8
        return 2 * away - (away // 4) * (4 * away - 15)

    a1 = lambda s: first_ring(s, z, dev_z, wa_in, lambda p: wa.at[y, p])
    b1 = lambda s: first_ring(s, y, dev_y, wb_in, lambda p: wb.at[z, p])
    a2 = lambda s, p: second_ring(s, p, y, dev_y, wa)
    b2 = lambda s, p: second_ring(s, p, z, dev_z, wb)

    right, left = (2 * ((x + 1) % NX) + c), (2 * ((x + 3) % NX) + c)
    opposite, sibling = (2 * ((x + 2) % NX) + c), (2 * x + 1 - c)

    def along_x_start(whole_in, half_in, half, whole):
        r0 = go(half_in(0), half(j, 0), dev_e(right))
        l1 = go(half_in(1), half(j, 1), dev_e(left))
        r1 = go(half_in(1), half(j, 1), dev_e(right))
        l0 = go(half_in(0), half(j, 0), dev_e(left))
        s = go(whole_in, whole(j), dev_e(sibling))
        return r0, l1, r1, l0, s

    def along_x_forward(first, half, whole):
        r0, l1, r1, l0, s = first
        r0.wait_recv()
        f0 = go(half(left, 0), half(left, 0), dev_e(right))
        l1.wait_recv()
        f1 = go(half(right, 1), half(right, 1), dev_e(left))
        return f0, f1, r1, l0, s

    def along_x_across(second, whole):
        f0, f1, r1, l0, s = second
        r1.wait_recv()
        s0 = go(whole(left), whole(left), dev_e(sibling))
        l0.wait_recv()
        s1 = go(whole(right), whole(right), dev_e(sibling))
        return f0, f1, s0, s1, s

    def along_x_last(second, half, whole):
        f0, f1, s0, s1, s = second
        f0.wait_recv()
        f1.wait_recv()
        s2 = go(whole(opposite), whole(opposite), dev_e(sibling))
        return s, s0, s1, s2

    f_half = lambda b, h: fg.at[b, pl.ds(64 * h, 64)]
    f_whole = lambda b: fg.at[b]
    w3 = lambda buf: (
        (lambda b, h: buf.at[pl.ds(3 * b, 3), pl.ds(32 * h, 32)]),
        (lambda b: buf.at[pl.ds(3 * b, 3)]),
    )
    e_half, e_whole = w3(eg)
    d_half, d_whole = w3(dg)

    ra, rb = a1(1), b1(1)
    fx = along_x_start(f_in, lambda h: f_in.at[pl.ds(64 * h, 64)], f_half, f_whole)
    ex = along_x_start(enc_in, lambda h: enc_in.at[:, pl.ds(32 * h, 32)], e_half, e_whole)

    wa[y, 0] = wa_in[...]
    wb[z, 0] = wb_in[...]
    fg[j] = f_in[...]
    eg[pl.ds(3 * j, 3)] = enc_in[...]
    dg[pl.ds(3 * j, 3)] = dec_in[...]
    nzg[j] = nz_in[...]
    ig[j] = ids_in[...]

    ring = []
    for step in (1, 2, 3, 4):
        arrive(ra)
        arrive(rb)
        if step < 4:
            ra, rb = a1(step + 1), b1(step + 1)
        if step != 3:
            piece = len(ring)
            ring.append((a2(1, piece), b2(1, piece)))
    fx = along_x_forward(fx, f_half, f_whole)

    def kv_part(b):
        rows = jnp.concatenate([wa[b, place_of(t, z)] for t in range(8)], axis=0)
        return mm(fg[b], rows)

    def code_of(p):
        level = jnp.where(code_row < 4, ids[p, 0, 2].astype(F32), ids[p, 0, 3].astype(F32))
        angle = level * freqs[...]
        return jnp.where((code_row & 2) == 0, jnp.sin(angle), jnp.cos(angle))

    def encode(g, carry):
        weights = jnp.concatenate([weights_of(eg, 2 * g), weights_of(eg, 2 * g + 1)], axis=0)
        enc = mm(four_spans(nzg, g), weights).astype(BF).astype(F32)
        for r in range(2):
            code = code_of(2 * g + r)
            for q in range(2):
                row = jnp.concatenate([code[4 * q + t : 4 * q + t + 1] for t in range(4)], axis=1)
                start = 128 * r + 64 * q
                hid[pl.ds(pl.multiple_of(g * 256 + start, 64), 64), :] = (enc[start : start + 64] + row).astype(BF)
        return carry

    def four_spans(buf, g):
        upper, lower = two_spans(buf[2 * g]), two_spans(buf[2 * g + 1])
        zero = jnp.zeros_like(upper)
        return jnp.concatenate(
            [jnp.concatenate([upper, zero], axis=1), jnp.concatenate([zero, lower], axis=1)], axis=0
        )

    def two_spans(pair):
        zero = jnp.zeros_like(pair)
        return jnp.concatenate([jnp.where(lane < STEPS, pair, zero), jnp.where(lane >= STEPS, pair, zero)], axis=0)

    def weights_of(buf, p):
        return jnp.concatenate([buf[ids[p, 0, 0]], buf[ids[p, 0, 1]]], axis=0)

    for step in (2, 3, 4):
        later = []
        for piece in range(3):
            for copies in ring[piece]:
                arrive(copies)
            later.append((a2(step, piece), b2(step, piece)))
        ring = later
        if step == 2:
            fx = along_x_across(fx, f_whole)
            ex = along_x_forward(ex, e_half, e_whole)
            dx = along_x_start(dec_in, lambda h: dec_in.at[:, pl.ds(32 * h, 32)], d_half, d_whole)
        if step == 3:
            fx = along_x_last(fx, f_half, f_whole)
            ex = along_x_across(ex, e_whole)
    arrive(small)
    table = pltpu.make_async_copy(ig, ids, local_sem)
    table.start()
    table.wait()
    arrive(fx)
    kv[:, 0:256] = kv_part(y)
    for step in (1, 2, 3):
        kv[:, 0:256] += kv_part((y - fwd * step + 16) % 8) + kv_part((y + fwd * step + 16) % 8)
    ex = along_x_last(ex, e_half, e_whole)
    arrive(ex)
    lax.fori_loop(0, 4, encode, 0)
    dx = along_x_forward(dx, d_half, d_whole)
    for piece in range(3):
        for copies in ring[piece]:
            arrive(copies)
    dx = along_x_across(dx, d_whole)
    kv[:, 0:256] += kv_part((y + 4) % 8)

    def kv_rest(b, total):
        return total + mm(fg[b], wb[:, place_of(b, y), 0:RK, :].reshape(8 * RK, 128))

    kv[:, 256:384] = lax.fori_loop(0, 8, kv_rest, jnp.zeros((GROUP * CTX, 128), F32))

    def unpack(zz, carry):
        for yy in range(NY):
            tiles = wb[zz, place_of(yy, y), RK:RB, :].astype(F32)
            qo[yy * NZ + zz] = jnp.concatenate([tiles[24 * r : 24 * r + 24] for r in range(3)], axis=1)
        return carry

    lax.fori_loop(0, NZ, unpack, 0)

    def split(b, carry):
        rows = qo[pl.ds(8 * b, 8)].reshape(HC, 2 * HC)
        wq[pl.ds(pl.multiple_of(HC * b, HC), HC), :] = rows[:, :HC].astype(BF)
        wo[pl.ds(pl.multiple_of(HC * b, HC), HC), :] = jnp.concatenate([rows[:, 256:], rows[:, HC:256]], axis=1).astype(BF)
        return carry

    lax.fori_loop(0, NY, split, 0)

    head_of_row = lax.broadcasted_iota(jnp.int32, (32, HC), 0) >> 3
    column = lax.broadcasted_iota(jnp.int32, (32, HC), 1)
    low = head_of_row * HD
    head_mask = jnp.where((column >= low) & (column < low + HD), 1.0, 0.0).astype(F32)

    def spread(flat):
        three = flat.astype(BF).astype(F32).reshape(GROUP, CTX, HC)
        return (jnp.concatenate([three] * 4, axis=1) * head_mask[None]).astype(BF)

    kb[...] = spread(kv[:, :HC])
    vb[...] = spread(kv[:, HC:])

    same_head = jnp.where(
        (lax.broadcasted_iota(jnp.int32, (128, 128), 0) >> 3)
        == (lax.broadcasted_iota(jnp.int32, (128, 128), 1) >> 3), 1.0, 0.0,
    ).astype(F32)
    same_span = (lax.broadcasted_iota(jnp.int32, (256, 128), 0) >> 6) == (
        lax.broadcasted_iota(jnp.int32, (256, 128), 1) >> 5
    )

    def four(buf, g):
        return buf[pl.ds(4 * g, 4)].reshape(128, HC)

    def head_sum(values):
        return jnp.dot(values, same_head, precision=lax.Precision.HIGHEST, preferred_element_type=F32)

    scale = 1.0 / math.sqrt(HD)

    def attend(g, carry):
        here = pl.ds(pl.multiple_of(256 * g, 256), 256)
        queries = mm(hid[here, :], wq[...]).astype(BF)
        scores = jnp.where(same_span, mm_nt(queries, four(kb, g)) * scale, 0.0)
        raised = jnp.exp(scores)
        probs = jnp.where(same_span, raised / head_sum(raised), 0.0)
        prs[here, :] = probs
        out = mm(probs.astype(BF), four(vb, g))
        att[here, :] = out.astype(BF)
        att_t[:, here] = out.T.astype(BF)
        return carry

    lax.fori_loop(0, 3, attend, 0)
    dx = along_x_last(dx, d_half, d_whole)
    lax.fori_loop(3, 4, attend, 0)
    arrive(dx)

    def four_decoders(g):
        return jnp.concatenate([weights_of(dg, 2 * g), weights_of(dg, 2 * g + 1)], axis=0)

    shares = []
    for k in (1, 2, 3, 0):
        g = (x + k) % NX
        here = pl.ds(pl.multiple_of(256 * g, 256), 256)
        branch = mm_nt(att[here, :], wo[...])
        if k == 0:
            row_pair = lax.broadcasted_iota(jnp.int32, (256, H), 0) >> 7
            branch += jnp.where(row_pair == c, hid[here, :].astype(F32), 0.0)
        product = mm_nt(branch.astype(BF), four_decoders(g))
        for r in range(2):
            block = product[128 * r : 128 * r + 128, 128 * r : 128 * r + 128]
            ps[2 * g + r] = jnp.where(lane < STEPS, block[0:STEPS], block[STEPS : 2 * STEPS]).astype(BF)
        for r in range(2):
            if k or r:
                p = 2 * g + (c + r) % 2
                shares.append(go(ps.at[p], pr.at[len(shares)], dev_e(p)))
    arrive(shares)
    predicted = ps[j].astype(F32)
    for k in range(1, ne):
        predicted += pr[k - 1].astype(F32)
    low_lane = lane[0:1] < STEPS
    length = jnp.where(low_lane, lengths[0].astype(F32), lengths[1].astype(F32))
    dims = jnp.where(low_lane, act_dims[emb_ids[0]].astype(F32), act_dims[emb_ids[1]].astype(F32))
    step_row = lax.broadcasted_iota(jnp.int32, (STEPS, 2 * STEPS), 0).astype(F32)
    step_col = (lane & (STEPS - 1)).astype(F32)
    valid = jnp.where((step_row < length) & (step_col < dims), 1.0, 0.0).astype(F32)
    error = predicted - vel_in[...]
    squares = jnp.sum(valid * error * error, axis=0, keepdims=True)
    sums = [jnp.sum(jnp.where(half_lanes, squares, 0.0), axis=1, keepdims=True) for half_lanes in (low_lane, ~low_lane)]
    one = [sums[q] / jnp.full((1, 1), lengths[q].astype(F32), F32) for q in range(2)]
    loss_out[...] = jnp.where(id_lane == 0, one[0], one[1])
    dp_own[...] = (2.0 * valid * error / length).astype(BF)
    errors = [go(dp_own, dpg.at[j], dev_e((j + k) % ne)) for k in range(1, ne)]
    dpg[j] = dp_own[...]
    arrive(errors)

    def d_branch(g, carry):
        dbr[pl.ds(pl.multiple_of(256 * g, 256), 256), :] = mm(four_spans(dpg, g), four_decoders(g)).astype(BF)
        return carry

    lax.fori_loop(0, 4, d_branch, 0)

    first_of = ((y, dev_y), (z, dev_z))

    def scatter(n, left_t, right_rows):
        for q in range(4):
            part = mm(left_t[...], right_rows[:, 384 * q : 384 * q + 384])
            wide[q] = part
            gs[n, q] = part.astype(BF)
        out = []
        for k in (4, 3, 5, 2, 6, 1, 7):
            for h, (me, device) in enumerate(first_of):
                t = (me + k) % 8
                rows = pl.ds(pl.multiple_of(96 * h + 48 * (t // 4), 16), 48)
                out.append(go(gs.at[n, t % 4, rows], gr.at[n, h, k - 1], device(t)))
        for h, (me, device) in enumerate(first_of):
            own_slice[n, h] = wide[me % 4, pl.ds(pl.multiple_of(96 * h + 48 * (me // 4), 16), 48), :]
        return out

    go_copies = scatter(1, att_t, dbr)

    def back(g, carry):
        here = pl.ds(pl.multiple_of(256 * g, 256), 256)
        d_att = mm(dbr[here, :], wo[...]).astype(BF)
        d_probs = mm_nt(d_att, four(vb, g))
        probs = prs[here, :]
        d_scores = (probs * (d_probs - head_sum(probs * d_probs))).astype(BF)
        out = mm(d_scores, four(kb, g)) * scale
        dq_t[:, here] = out.T.astype(BF)
        return carry

    lax.fori_loop(0, 4, back, 0)
    gq_copies = scatter(0, dq_t, hid)

    def add_up(n, copies):
        arrive(copies)
        out = []
        for h in range(2):
            total = own_slice[n, h]
            for k in range(7):
                total += gr[n, h, k].astype(F32)
            for t in range(9):
                sb[n, h, t] = total[16 * (t // 3) : 16 * (t // 3) + 16, 128 * (t % 3) : 128 * (t % 3) + 128].astype(BF)
            me, device = first_of[1 - h]
            for k in range(1, 8):
                t = (me + k) % 8
                out.append(go(sb.at[n, h, pl.ds(2 * t, 2)], sr.at[n, h, k - 1], device(t)))
        return out

    def finish(n, copies):
        arrive(copies)
        out = []
        for h in range(2):
            me, device = first_of[1 - h]
            total = sb[n, h, pl.ds(2 * me, 2)].astype(F32)
            for k in range(7):
                total += sr[n, h, k].astype(F32)
            fs[n, h] = total.astype(BF)
            out += [go(fs.at[n, h], sg.at[n, h, pl.ds(2 * me, 2)], device((me + k) % 8)) for k in range(1, 8)]
            sg[n, h, pl.ds(2 * me, 2)] = fs[n, h]
        return out

    def gather(n, copies):
        arrive(copies)
        out = []
        for h, (me, device) in enumerate(first_of):
            sent = [
                go(sg.at[n, h, pl.ds(0, 9)], og.at[n, h, me], device((me + fwd * k + 8) % 8)) for k in (2, -2, 1, -1)
            ]
            og[n, h, me] = sg[n, h, 0:9]
            out.append(sent)
        return out

    def gather_on(n, before):
        out = []
        for h, (me, device) in enumerate(first_of):
            ahead, behind, *near = before[h]
            ahead.wait_recv()
            block = og.at[n, h, (me - 2 * fwd + 8) % 8]
            out += [go(block, block, device((me + fwd * k + 8) % 8)) for k in (2, 1)]
            behind.wait_recv()
            block = og.at[n, h, (me + 2 * fwd + 8) % 8]
            out.append(go(block, block, device((me - fwd + 8) % 8)))
            out += near
        return out

    def write(n, out):
        for h in range(2):
            for t in range(8):
                for r in range(9):
                    row, column = 96 * h + 48 * (t // 4) + 16 * (r // 3), 384 * (t % 4) + 128 * (r % 3)
                    out[row : row + 16, column : column + 128] = og[n, h, t, r]

    sb[:, :, 9:16] = jnp.zeros((2, 2, 7, 16, 128), BF)
    go_copies = add_up(1, go_copies)
    go_copies = finish(1, go_copies)
    gq_copies = add_up(0, gq_copies)
    go_copies = gather(1, go_copies)
    gq_copies = finish(0, gq_copies)
    go_copies = gather_on(1, go_copies)
    gq_copies = gather(0, gq_copies)
    arrive(go_copies)
    gq_copies = gather_on(0, gq_copies)
    write(1, go_out)
    arrive(gq_copies)
    write(0, gq_out)
    for copy in cs.made:
        copy.wait_send()


def widen(q_in, o_in, loss_in, q_out, o_out, loss_out):
    q_out[...] = q_in[...].astype(F32)
    o_out[...] = o_in[...].astype(F32)
    for q in range(2):
        loss_out[q] = loss_in[0, q]


def body(actions, noise, emb_ids, lengths, t_index, act_dims, features, enc_w, dec_w, wq, wk, wv, wo_t):
    vm = pl.BlockSpec(memory_space=pltpu.VMEM)
    sm = pl.BlockSpec(memory_space=pltpu.SMEM)
    V = pltpu.VMEM
    d_q, d_o, loss = pl.pallas_call(
        kernel,
        out_shape=(
            jax.ShapeDtypeStruct((HC, H), BF),
            jax.ShapeDtypeStruct((HC, H), BF),
            jax.ShapeDtypeStruct((8, 128), F32),
        ),
        in_specs=[vm] * 2 + [sm] * 4 + [vm] * 7,
        out_specs=(vm, vm, vm),
        scratch_shapes=[
            V((RK, 256), BF),
            V((RB, 128), BF),
            V((STEPS, 128), BF),
            V((STEPS, 128), F32),
            V((8, 384), F32),
            V((8, 128), jnp.int32),
            V((NY, NZ, RK, 256), BF),
            V((NZ, NY, RB, 128), BF),
            V((8, GROUP * CTX, 640), BF),
            V((EMBS, STEPS, H), BF),
            V((EMBS, STEPS, H), BF),
            V((8, STEPS, 128), BF),
            V((8, 8, 128), jnp.int32),
            pltpu.SMEM((8, 8, 128), jnp.int32),
            V((GROUP * CTX, 2 * HC), F32),
            V((64, 24, 2 * HC), F32),
            V((H, HC), BF),
            V((H, HC), BF),
            V((GROUP, 32, HC), BF),
            V((GROUP, 32, HC), BF),
            V((ROWS, H), BF),
            V((ROWS, H), BF),
            V((ROWS, 128), F32),
            V((ROWS, HC), BF),
            V((HC, ROWS), BF),
            V((HC, ROWS), BF),
            V((8, STEPS, 128), BF),
            V((7, STEPS, 128), BF),
            V((STEPS, 128), BF),
            V((8, STEPS, 128), BF),
            V((2, 4, HC, 384), BF),
            V((4, HC, 384), F32),
            V((2, 2, 48, 384), F32),
            V((2, 2, 7, 48, 384), BF),
            V((2, 2, 16, 16, 128), BF),
            V((2, 2, 7, 2, 16, 128), BF),
            V((2, 2, 2, 16, 128), BF),
            V((2, 2, 16, 16, 128), BF),
            V((2, 2, 8, 9, 16, 128), BF),
            pltpu.SemaphoreType.DMA((N_COPIES,)),
            pltpu.SemaphoreType.DMA((N_COPIES,)),
            pltpu.SemaphoreType.DMA,
        ],
        compiler_params=pltpu.CompilerParams(
            collective_id=0, has_side_effects=True, vmem_limit_bytes=56 * 1024 * 1024
        ),
    )(
        actions, noise, emb_ids, lengths, t_index, act_dims, features.reshape(GROUP * CTX, 640), enc_w,
        jnp.swapaxes(dec_w, 1, 2), wq, wk, wv, wo_t,
    )
    return pl.pallas_call(
        widen,
        out_shape=(
            jax.ShapeDtypeStruct((HC, H), F32), jax.ShapeDtypeStruct((HC, H), F32), jax.ShapeDtypeStruct((2,), F32),
        ),
        in_specs=[vm, vm, sm],
        out_specs=(vm, vm, sm),
    )(d_q, d_o, loss)


def solution(mesh):
    rows = P(("dp", "emb"))
    in_specs = (
        P(("dp", "emb"), None, None), P(("dp", "emb"), None, None), rows, rows, rows, P(),
        P("dp", None, "emb"), P("emb", None, None), P("emb", None, None),
        P("dp", "emb"), P("dp", "emb"), P("dp", "emb"), P("dp", "emb"),
    )
    out_specs = (P("emb", None), P("emb", None), rows)
    return jax.shard_map(body, mesh=mesh, in_specs=in_specs, out_specs=out_specs, check_vma=False)
```
